128 devices in a mesh: grp: 4 (over z), sub: 32 (over x, y, core).
Axes of the slice: x: 4, y: 4, z: 4, core: 2. Of those that a mesh axis runs over, the one named last changes fastest.
Arguments:
- deformation_vector: float32 [3, 128, 1024, 256], P(None, 'grp', 'sub'), may hold values from -6 to 6
- heating_traction: float32 [3, 128, 1024, 256], P(None, 'grp', 'sub'), may hold values from -6 to 6
- heat_level: float32 [128, 1024, 256], P('grp', 'sub'), may hold values from 0 to 1
- substance_label: int32 [128, 1024, 256], P('grp', 'sub'), may hold values from 0 to 3
- substance_stiffness_list: float32 [4, 2], replicated, may hold values from 0.3 to 3
- subregion_spans: int32 [4, 32], P('grp', 'sub'), may hold values from 64 to 256, as said below
- projection_basis: bfloat16 [8, 3, 128, 1024, 256], P(None, None, 'grp', 'sub'), may hold values from -0.0068359375 to 0.0068359375
- reduced_system_reciprocal: float32 [1024, 1024], P(('grp', 'sub')), may hold values from -1 to 1
Outputs:
- displacement_next: float32 [3, 128, 1024, 256], P(None, 'grp', 'sub')
- residual: float32 [3, 128, 1024, 256], P(None, 'grp', 'sub')
- coarse_update: float32 [1024], P(('grp', 'sub'))
The draws below stay inside these ranges and needn't reach their ends.
Inputs may be any that keep to these rules, and one draw needn't show every extreme that they name: `subregion_spans`: some subdomain is active along its whole third dimension.
All inputs are finite; a program needn't handle non-finite values.
Results may differ from the reference program's by a relative error of at most 0.003.
Values sent between devices are 32-bit elements; how exact they have to be, the bound alone decides.
A program may use at most 128 MiB of HBM per device.

```python
import math
import jax
import jax.numpy as jnp
from jax import lax

CX = 32
CY = 32
CZ = 256
SWEEPS = 2
KVEC = 8
NMAT = 4
LENGTH_ROWS_X = 128
LENGTH_ROWS_Y = 1024
LENGTH_ROWS_Z = 256
NCOARSE = 1024
N_GRP = 4
N_SUB = 32


def draw_subregion_spans(key, part):
    first = jax.random.fold_in(key, 11)
    second = jax.random.fold_in(key, 12)
    count = N_GRP * N_SUB
    values = jax.random.randint(first, (count,), CZ // 4, CZ + 1, dtype=jnp.int32)
    chosen = jax.random.randint(second, (), 0, count, dtype=jnp.int32)
    values = jnp.where(jnp.arange(count, dtype=jnp.int32) == chosen, CZ, values)
    return values.reshape(N_GRP, N_SUB)


def draw_reduced_system_reciprocal(key, part):
    inner_key = jax.random.fold_in(key, 21)
    noise = jnp.clip(jax.random.normal(inner_key, (NCOARSE, NCOARSE), jnp.float32), -6.0, 6.0)
    rows = lax.broadcasted_iota(jnp.int32, (NCOARSE, NCOARSE), 0)
    columns = lax.broadcasted_iota(jnp.int32, (NCOARSE, NCOARSE), 1)
    diagonal = jnp.where(rows == columns, 0.2, 0.0).astype(jnp.float32)
    return noise * (0.1 / math.sqrt(NCOARSE)) + diagonal


def touch_ends(values, own_key, smallest, top_value):
    index_at = [jax.random.randint(jax.random.fold_in(own_key, axis), (), 0, length) for axis, length in enumerate(values.shape)]
    longest = values.shape.index(max(values.shape))
    next_to = index_at[:longest] + [(index_at[longest] + 1) % values.shape[longest]] + index_at[longest + 1:]
    return values.at[tuple(index_at)].set(smallest).at[tuple(next_to)].set(top_value)


def shard_levels(own_key, shape, pieces, least, top_value):
    factor_of = 1.0
    for axis_at, parts in pieces:
        heights = jax.random.uniform(jax.random.fold_in(jax.random.fold_in(own_key, 6), axis_at), (parts,), jnp.float32, least / len(pieces), top_value / len(pieces))
        factor_of = factor_of * jnp.repeat(jnp.exp(heights), shape[axis_at] // parts).reshape((-1,) + (1,) * (len(shape) - 1 - axis_at))
    return factor_of


def scatter_about(stream_key, shape, scale, bound, split=(), held_as=jnp.bfloat16):
    entries = scale * jax.random.normal(stream_key, shape, jnp.float32)
    if split:
        entries = entries * shard_levels(stream_key, shape, split, -0.22, 0.18)
    return jnp.clip(entries, -bound, bound).astype(held_as)


def setup_inputs(seed: int = 0) -> dict:
    splits = jax.random.split(jax.random.key(seed), 9)
    return {
        "deformation_vector": scatter_about(splits[0], (3, LENGTH_ROWS_X, LENGTH_ROWS_Y, LENGTH_ROWS_Z), 1.0, 6.0, ((1, 4), (2, 32)), jnp.float32),
        "heating_traction": scatter_about(splits[1], (3, LENGTH_ROWS_X, LENGTH_ROWS_Y, LENGTH_ROWS_Z), 1.0, 6.0, ((1, 4), (2, 32)), jnp.float32),
        "heat_level": jnp.clip(1.0 * jax.random.uniform(splits[2], (LENGTH_ROWS_X, LENGTH_ROWS_Y, LENGTH_ROWS_Z), jnp.float32) ** shard_levels(splits[2], (LENGTH_ROWS_X, LENGTH_ROWS_Y, LENGTH_ROWS_Z), ((0, 4), (1, 32)), -0.2, 0.2), 0.0, 1.0),
        "substance_label": touch_ends(jax.random.randint(splits[3], (LENGTH_ROWS_X, LENGTH_ROWS_Y, LENGTH_ROWS_Z), 0, NMAT), jax.random.fold_in(splits[3], 1), 0, NMAT - 1).astype(jnp.int32),
        "substance_stiffness_list": jnp.clip(jnp.exp(jax.random.uniform(splits[4], (NMAT, 2), jnp.float32, math.log(0.3), math.log(3.0))), 0.3, 3.0),
        "subregion_spans": draw_subregion_spans(jax.random.fold_in(splits[8], 71), 0),
        "projection_basis": scatter_about(splits[6], (KVEC, 3, LENGTH_ROWS_X, LENGTH_ROWS_Y, LENGTH_ROWS_Z), (3 * CX * CY * CZ) ** -0.5, 0.0068359375, ((2, 4), (3, 32))),
        "reduced_system_reciprocal": draw_reduced_system_reciprocal(jax.random.fold_in(splits[8], 71), 0),
    }


SHIFT = 1.0
ROBIN = 1.0
OMEGA = 0.6
UNITS = ((1, 0, 0), (0, 1, 0), (0, 0, 1))


def combine(first, second, sign):
    return tuple(left + sign * right for left, right in zip(first, second))


def negate(first):
    return tuple(-left for left in first)


def stencil(padded, rigidity_amount, lambda_stiffness):
    size_x, size_y, size_z = rigidity_amount.shape

    def pick(component, offset):
        return padded[component, 1 + offset[0]:1 + offset[0] + size_x, 1 + offset[1]:1 + offset[1] + size_y, 1 + offset[2]:1 + offset[2] + size_z]

    results = []
    for component in range(3):
        center = pick(component, (0, 0, 0))
        laplace = -6.0 * center
        graddiv = jnp.zeros_like(center)
        for direction in range(3):
            forward = pick(component, UNITS[direction])
            backward = pick(component, negate(UNITS[direction]))
            laplace = laplace + forward + backward
            if direction == component:
                graddiv = graddiv + (forward + backward - 2.0 * center)
            else:
                own_unit = UNITS[component]
                other = UNITS[direction]
                cross = pick(direction, combine(own_unit, other, 1)) - pick(direction, combine(own_unit, other, -1))
                cross = cross - pick(direction, combine(negate(own_unit), other, 1)) + pick(direction, combine(negate(own_unit), other, -1))
                graddiv = graddiv + 0.25 * cross
        results.append(SHIFT * center - rigidity_amount * laplace - (lambda_stiffness + rigidity_amount) * graddiv)
    return jnp.stack(results)


def operate(field, rigidity_amount, lambda_stiffness):
    return stencil(jnp.pad(field, ((0, 0), (1, 1), (1, 1), (1, 1))), rigidity_amount, lambda_stiffness)


def block_masks(shape, width):
    index_x = lax.broadcasted_iota(jnp.int32, shape, 0)
    index_y = lax.broadcasted_iota(jnp.int32, shape, 1)
    inner = (index_x >= 1) & (index_x <= shape[0] - 2) & (index_y >= 1) & (index_y <= shape[1] - 2)
    edge = (index_x == 1) | (index_x == shape[0] - 2) | (index_y == 1) | (index_y == shape[1] - 2)
    rim = jnp.where(inner & edge, 1.0, 0.0).astype(jnp.float32)
    return inner, rim


def stiffness_constants(substance_label, heat_level, stiffness_lookup, enabled_marker):
    rigidity_amount = jnp.zeros(substance_label.shape, jnp.float32)
    lambda_stiffness = jnp.zeros(substance_label.shape, jnp.float32)
    for index in range(stiffness_lookup.shape[0]):
        rigidity_amount = jnp.where(substance_label == index, stiffness_lookup[index, 0], rigidity_amount)
        lambda_stiffness = jnp.where(substance_label == index, stiffness_lookup[index, 1], lambda_stiffness)
    weakening_multiplier = 2.0 - heat_level
    rigidity_amount = jnp.where(enabled_marker, rigidity_amount * weakening_multiplier, 0.0)
    lambda_stiffness = jnp.where(enabled_marker, lambda_stiffness * weakening_multiplier, 0.0)
    return rigidity_amount, lambda_stiffness


def solve_direct(state, width):
    started = state[0:3]
    forcing = state[3:6]
    rigidity_amount = state[6]
    lambda_stiffness = state[7]
    inner, rim = block_masks(rigidity_amount.shape, width)
    update = inner & (rigidity_amount > 0)
    scale = SHIFT + 8.0 * rigidity_amount + 2.0 * lambda_stiffness + ROBIN * rim
    field = started
    for sweep_step in range(width):
        defect = forcing - operate(field, rigidity_amount, lambda_stiffness) - ROBIN * rim * (field - started)
        field = jnp.where(update, field + OMEGA * defect / scale, field)
    return field[:, width:-width, width:-width, :]


def reference(deformation_vector, heating_traction, heat_level, substance_label, substance_stiffness_list, subregion_spans, projection_basis, reduced_system_reciprocal):
    count = N_GRP * N_SUB
    extent_full = jnp.repeat(jnp.repeat(subregion_spans, CX, axis=0), CY, axis=1)
    depth = lax.broadcasted_iota(jnp.int32, substance_label.shape, 2)
    enabled_marker = depth < extent_full[:, :, None]
    rigidity_amount, lambda_stiffness = stiffness_constants(substance_label, heat_level, substance_stiffness_list, enabled_marker)
    started = jnp.where(enabled_marker, deformation_vector, 0.0)
    forcing = jnp.where(enabled_marker, heating_traction, 0.0)
    state = jnp.concatenate([started, forcing, rigidity_amount[None], lambda_stiffness[None]], axis=0)
    padded = jnp.pad(state, ((0, 0), (SWEEPS, SWEEPS), (SWEEPS, SWEEPS), (0, 0)))
    zero = jnp.zeros((), jnp.int32)

    def local(index):
        group = (index // N_SUB).astype(jnp.int32)
        member = (index % N_SUB).astype(jnp.int32)
        block = lax.dynamic_slice(padded, (zero, group * CX, member * CY, zero), (8, CX + 2 * SWEEPS, CY + 2 * SWEEPS, LENGTH_ROWS_Z))
        return solve_direct(block, SWEEPS)

    blocks = lax.map(local, jnp.arange(count, dtype=jnp.int32))
    moved = blocks.reshape(N_GRP, N_SUB, 3, CX, CY, LENGTH_ROWS_Z).transpose(2, 0, 3, 1, 4, 5).reshape(3, LENGTH_ROWS_X, LENGTH_ROWS_Y, LENGTH_ROWS_Z)
    residual = jnp.where(enabled_marker, forcing - operate(moved, rigidity_amount, lambda_stiffness), 0.0)
    residual_half = residual.astype(jnp.bfloat16)

    def project(index):
        group = (index // N_SUB).astype(jnp.int32)
        member = (index % N_SUB).astype(jnp.int32)
        vectors = lax.dynamic_slice(projection_basis, (zero, zero, group * CX, member * CY, zero), (KVEC, 3, CX, CY, LENGTH_ROWS_Z))
        piece = lax.dynamic_slice(residual_half, (zero, group * CX, member * CY, zero), (3, CX, CY, LENGTH_ROWS_Z))
        return jnp.dot(vectors.reshape(KVEC, -1), piece.reshape(-1), preferred_element_type=jnp.float32)

    coarse_residual = lax.map(project, jnp.arange(count, dtype=jnp.int32)).reshape(NCOARSE)
    coarse_update = jnp.dot(reduced_system_reciprocal, coarse_residual, precision=lax.Precision.HIGHEST)
    return moved, residual, coarse_update
```

```python
import functools

import jax
import jax.numpy as jnp
from jax import lax
from jax.experimental import pallas as pl
from jax.experimental.pallas import tpu as pltpu
from jax.sharding import PartitionSpec as P

SHIFT = 1.0
ROBIN = 1.0
OMEGA = 0.6
MESH = pl.DeviceIdType.MESH

NX = 32
NY = 32
ROWS = 48
FIRST = 8
F32 = jnp.float32


def each(op, *pairs):
    return [op(*parts) for parts in zip(*pairs)]


def add(left, right):
    return each(lambda p, q: p + q, left, right)


def sub(left, right):
    return each(lambda p, q: p - q, left, right)


def mul(left, right):
    return each(lambda p, q: p * q, left, right)


def scaled(factor, pair):
    return [factor * part for part in pair]


def shifts(pair, lane):
    low, high = pair
    last = lane == 127
    first = lane == 0
    low_up = pltpu.roll(low, 127, 1)
    high_up = pltpu.roll(high, 127, 1)
    low_down = pltpu.roll(low, 1, 1)
    high_down = pltpu.roll(high, 1, 1)
    up = [jnp.where(last, high_up, low_up), jnp.where(last, 0.0, high_up)]
    down = [jnp.where(first, 0.0, low_down), jnp.where(first, low_down, high_down)]
    return up, down


def gap(pair, lane):
    up, down = shifts(pair, lane)
    return sub(up, down)


def block(field, forcing, mu, beta, x, yb, lane):
    row = FIRST + 8 * yb

    def at(component, dx, dy):
        return [field[component, x + 1 + dx, half, pl.ds(row + dy, 8), :] for half in (0, 1)]

    def own(ref):
        return [ref[x, pl.ds(8 * yb, 8), pl.ds(128 * half, 128)] for half in (0, 1)]

    shear, mixed = own(mu), own(beta)
    centre, ahead, behind, above, below = ([at(c, *o) for c in range(3)] for o in ((0, 0), (1, 0), (-1, 0), (0, 1), (0, -1)))
    turn = sub(ahead[0], behind[0])
    twist = sub(above[1], below[1])
    cross = [
        add(
            sub(sub(at(1, 1, 1), at(1, 1, -1)), sub(at(1, -1, 1), at(1, -1, -1))),
            gap(sub(ahead[2], behind[2]), lane),
        ),
        add(
            sub(sub(at(0, 1, 1), at(0, 1, -1)), sub(at(0, -1, 1), at(0, -1, -1))),
            gap(sub(above[2], below[2]), lane),
        ),
        gap(add(turn, twist), lane),
    ]
    defects = []
    for c in range(3):
        up, down = shifts(centre[c], lane)
        double = scaled(2.0, centre[c])
        seconds = [
            sub(add(ahead[c], behind[c]), double),
            sub(add(above[c], below[c]), double),
            sub(add(up, down), double),
        ]
        laplace = add(add(seconds[0], seconds[1]), seconds[2])
        graddiv = add(seconds[c], scaled(0.25, cross[c]))
        force = [forcing[c, x, pl.ds(8 * yb, 8), pl.ds(128 * half, 128)] for half in (0, 1)]
        defects.append(add(sub(force, centre[c]), add(mul(shear, laplace), mul(mixed, graddiv))))
    return centre, defects, shear, mixed


def kernel(
    deformation,
    traction,
    heat_level,
    label,
    table,
    span,
    basis,
    reciprocal,
    moved,
    residual,
    coarse,
    v0,
    v1,
    v2,
    force,
    heat,
    kind,
    mu,
    beta,
    kappa,
    vectors,
    rows_r,
    rimmed,
    side_send,
    side_recv,
    corner_send,
    corner_recv,
    total,
    line,
    near,
    far,
    load_sem,
    face_ss,
    face_rs,
    side_ss,
    side_rs,
    corner_ss,
    corner_rs,
    near_ss,
    near_rs,
    far_ss,
    far_rs,
):
    grp = lax.axis_index("grp")
    sub_at = lax.axis_index("sub")
    place = lax.rem(sub_at, 8)
    column = lax.div(sub_at, 8)
    cell = grp * 4 + column

    loads = [
        pltpu.make_async_copy(
            deformation.at[:, :, :, pl.ds(128 * half, 128)],
            v0.at[:, pl.ds(1, NX), half, pl.ds(FIRST, NY), :],
            load_sem.at[half],
        )
        for half in (0, 1)
    ]
    heat_load = pltpu.make_async_copy(heat_level, heat, load_sem.at[2])
    kind_load = pltpu.make_async_copy(label, kind, load_sem.at[3])
    force_load = pltpu.make_async_copy(traction, force, load_sem.at[4])
    rows_load = pltpu.make_async_copy(reciprocal, rows_r, load_sem.at[5])
    basis_load = pltpu.make_async_copy(basis, vectors, load_sem.at[6])
    for load in loads:
        load.start()
    heat_load.start()
    kind_load.start()
    force_load.start()

    def shifted(dx, dy):
        return (lax.rem(grp + 4 + dx, 4), lax.rem(sub_at + 32 + dy, 32))

    def near_peer(step):
        return (grp, column * 8 + lax.rem(place + step, 8))

    def far_peer(step):
        other = lax.rem(cell + step, 16)
        return (lax.div(other, 4), lax.rem(other, 4) * 8 + place)

    corners = ((-1, -1), (-1, 1), (1, -1), (1, 1))
    barrier = pltpu.get_barrier_semaphore()
    partners = [shifted(-1, 0), shifted(1, 0), shifted(0, -1), shifted(0, 1)]
    partners += [shifted(*corner) for corner in corners]
    partners += [near_peer(step) for step in range(1, 8)]
    partners += [far_peer(step) for step in range(1, 16)]
    for partner in partners:
        pl.semaphore_signal(barrier, inc=1, device_id=partner, device_id_type=MESH)

    lane = lax.broadcasted_iota(jnp.int32, (8, 128), 1)
    reach = span[0, 0]
    active = [lane < reach, lane + 128 < reach]

    def messages(round_at, field, low_face, high_face):
        found = []
        for side, dx in enumerate((-1, 1)):
            source = (low_face, high_face)[side]
            found.append(
                pltpu.make_async_remote_copy(
                    src_ref=source,
                    dst_ref=field.at[:, 33 if dx < 0 else 0, :, pl.ds(FIRST, NY), :],
                    send_sem=face_ss.at[round_at, side],
                    recv_sem=face_rs.at[round_at, side],
                    device_id=shifted(dx, 0),
                    device_id_type=MESH,
                )
            )
        for side, dy in enumerate((-1, 1)):
            found.append(
                pltpu.make_async_remote_copy(
                    src_ref=side_send.at[round_at, side],
                    dst_ref=side_recv.at[round_at, 1 - side],
                    send_sem=side_ss.at[round_at, side],
                    recv_sem=side_rs.at[round_at, side],
                    device_id=shifted(0, dy),
                    device_id_type=MESH,
                )
            )
        for number, corner in enumerate(corners):
            found.append(
                pltpu.make_async_remote_copy(
                    src_ref=corner_send.at[round_at, number],
                    dst_ref=corner_recv.at[round_at, 3 - number],
                    send_sem=corner_ss.at[round_at, number],
                    recv_sem=corner_rs.at[round_at, number],
                    device_id=shifted(*corner),
                    device_id_type=MESH,
                )
            )
        return found

    inside = [
        jnp.where(flag, 1.0, 0.0).astype(F32) for flag in (grp > 0, grp < 3, sub_at > 0, sub_at < 31)
    ]

    def pack_corners(round_at, take):
        for number, (dx, dy) in enumerate(corners):
            for c in range(3):
                for half in (0, 1):
                    corner_send[round_at, number, pl.ds(2 * c + half, 1), :] = take(dx, dy, c, half)

    def unpack(round_at, field):
        for c in range(3):
            for half in (0, 1):
                for number, (dx, dy) in enumerate(corners):
                    keep = inside[0 if dx < 0 else 1] * inside[2 if dy < 0 else 3]
                    field[c, 0 if dx < 0 else 33, half, pl.ds(7 if dy < 0 else 40, 1), :] = (
                        corner_recv[round_at, number, pl.ds(2 * c + half, 1), :] * keep
                    )

        @pl.loop(0, NX)
        def _(x):
            for side in (0, 1):
                for c in range(3):
                    for half in (0, 1):
                        field[c, x + 1, half, pl.ds(7 if side == 0 else 40, 1), :] = (
                            side_recv[round_at, side, c, half, pl.ds(x, 1), :] * inside[2 + side]
                        )

        for side in (0, 1):

            @pl.when(grp == (0 if side == 0 else 3))
            def _():
                field[:, 0 if side == 0 else 33, :, pl.ds(FIRST, NY), :] = jnp.zeros((3, 2, NY, 128), F32)

    def pack_side(round_at, field, x):
        for side in (0, 1):
            for c in range(3):
                for half in (0, 1):
                    side_send[round_at, side, c, half, pl.ds(x, 1), :] = field[
                        c, x + 1, half, pl.ds(FIRST if side == 0 else FIRST + NY - 1, 1), :
                    ]

    def field_corner(field):
        return lambda dx, dy, c, half: field[
            c, 1 if dx < 0 else NX, half, pl.ds(FIRST if dy < 0 else FIRST + NY - 1, 1), :
        ]

    def faces(field):
        return (
            field.at[:, 1, :, pl.ds(FIRST, NY), :],
            field.at[:, NX, :, pl.ds(FIRST, NY), :],
        )

    for load in loads:
        load.wait()
    basis_load.start()
    rows_load.start()

    @pl.loop(0, NX)
    def _(x):
        for c in range(3):
            for half in (0, 1):
                for yb in range(4):
                    rows = pl.ds(FIRST + 8 * yb, 8)
                    v0[c, x + 1, half, rows, :] = jnp.where(active[half], v0[c, x + 1, half, rows, :], 0.0)
        pack_side(0, v0, x)

    pack_corners(0, field_corner(v0))
    pl.semaphore_wait(barrier, len(partners))
    first = messages(0, v0, *faces(v0))
    for message in first:
        message.start()

    heat_load.wait()
    kind_load.wait()
    force_load.wait()

    @pl.loop(0, NX)
    def _(x):
        for yb in range(4):
            for half in (0, 1):
                at = (x, pl.ds(8 * yb, 8), pl.ds(128 * half, 128))
                material = kind[at]
                shear = jnp.full((8, 128), table[0, 0], F32)
                lame = jnp.full((8, 128), table[0, 1], F32)
                for number in range(1, 4):
                    chosen = material == number
                    shear = jnp.where(chosen, table[number, 0], shear)
                    lame = jnp.where(chosen, table[number, 1], lame)
                weakening = jnp.where(active[half], 2.0 - heat[at], 0.0)
                shear = shear * weakening
                mixed = lame * weakening + shear
                mu[at] = shear
                beta[at] = mixed
                kappa[at] = OMEGA / (SHIFT + 6.0 * shear + 2.0 * mixed)
                for c in range(3):
                    force[(c,) + at] = jnp.where(active[half], force[(c,) + at], 0.0)

    for message in first:
        message.wait_recv()
    unpack(0, v0)

    def sweep_block(source, target, x, yb, also_out):
        centre, defects, shear, mixed = block(source, force, mu, beta, x, yb, lane)
        step = [kappa[x, pl.ds(8 * yb, 8), pl.ds(128 * half, 128)] for half in (0, 1)]
        for c in range(3):
            new = add(centre[c], mul(step, defects[c]))
            for half in (0, 1):
                target[c, x + 1, half, pl.ds(FIRST + 8 * yb, 8), :] = new[half]
                if also_out:
                    moved[c, x, pl.ds(8 * yb, 8), pl.ds(128 * half, 128)] = new[half]
        return centre, defects, shear, mixed

    def first_edge(x, yb):
        slot = jnp.where(x == 0, 0, jnp.where(x == NX - 1, 1, 2))
        centre, defects, shear, mixed = sweep_block(v0, v1, x, yb, False)
        step = each(lambda p, q: OMEGA / (SHIFT + ROBIN + 6.0 * p + 2.0 * q), shear, mixed)
        for c in range(3):
            new = add(centre[c], mul(step, defects[c]))
            for half in (0, 1):
                rimmed[slot, c, half, pl.ds(8 * yb, 8), :] = new[half]

    @pl.loop(0, 2)
    def _(end):
        for yb in (1, 2):
            first_edge(end * (NX - 1), yb)

    @pl.loop(0, NX)
    def _(x):
        slot = jnp.where(x == 0, 0, jnp.where(x == NX - 1, 1, 2))
        for yb in (0, 3):
            first_edge(x, yb)
        for side in (0, 1):
            for c in range(3):
                for half in (0, 1):
                    side_send[1, side, c, half, pl.ds(x, 1), :] = rimmed[
                        slot, c, half, pl.ds(0 if side == 0 else NY - 1, 1), :
                    ]

    pack_corners(
        1,
        lambda dx, dy, c, half: rimmed[
            0 if dx < 0 else 1, c, half, pl.ds(0 if dy < 0 else NY - 1, 1), :
        ],
    )
    second = messages(1, v1, rimmed.at[0], rimmed.at[1])
    for message in second:
        message.start()

    @pl.loop(1, NX - 1)
    def _(x):
        for yb in (1, 2):
            sweep_block(v0, v1, x, yb, False)

    @pl.loop(1, NX - 1)
    def _(x):
        for yb in (1, 2):
            sweep_block(v1, v2, x, yb, True)

    for message in second:
        message.wait_recv()
    unpack(1, v1)

    @pl.loop(0, 2)
    def _(end):
        for yb in (1, 2):
            sweep_block(v1, v2, end * (NX - 1), yb, True)

    @pl.loop(0, NX)
    def _(x):
        for yb in (0, 3):
            sweep_block(v1, v2, x, yb, True)
        pack_side(2, v2, x)

    pack_corners(2, field_corner(v2))
    third = messages(2, v2, *faces(v2))
    for message in third:
        message.start()

    def residual_block(x, yb):
        _, defects, _, _ = block(v2, force, mu, beta, x, yb, lane)
        for c in range(3):
            for half in (0, 1):
                residual[c, x, pl.ds(8 * yb, 8), pl.ds(128 * half, 128)] = defects[c][half]

    @pl.loop(1, NX - 1)
    def _(x):
        for yb in (1, 2):
            residual_block(x, yb)

    for message in third:
        message.wait_recv()
    unpack(2, v2)
    basis_load.wait()
    total[...] = jnp.zeros_like(total)

    @pl.loop(0, 2)
    def _(end):
        for yb in (1, 2):
            residual_block(end * (NX - 1), yb)

    @pl.loop(0, NX)
    def _(x):
        for yb in (0, 3):
            residual_block(x, yb)
        part = total[...]
        for c in range(3):
            half_way = residual[c, x].astype(jnp.bfloat16)
            plane = vectors[:, c, x].reshape(8 * NY, 256)
            part += lax.dot_general(
                half_way, plane, (((1,), (1,)), ((), ())), preferred_element_type=F32
            )
        total[...] = part

    own_row = lax.broadcasted_iota(jnp.int32, (NY, 256), 0)
    of_lane = lax.broadcasted_iota(jnp.int32, (NY, 256), 1)
    kept = jnp.where(lax.rem(of_lane, NY) == own_row, total[...], 0.0)
    folded = kept[0:8] + kept[8:16] + kept[16:24] + kept[24:32]
    source_lane = lax.broadcasted_iota(jnp.int32, (256, 128), 0)
    target_lane = lax.broadcasted_iota(jnp.int32, (256, 128), 1)
    start_lane = 64 * lax.rem(cell, 2) + 8 * place
    pick = jnp.where(start_lane + lax.div(source_lane, NY) == target_lane, 1.0, 0.0).astype(F32)
    spread = jnp.dot(folded, pick, preferred_element_type=F32, precision=lax.Precision.HIGHEST)
    line[0] = jnp.sum(spread, axis=0, keepdims=True)

    hops = [
        pltpu.make_async_remote_copy(
            src_ref=line.at[0],
            dst_ref=near.at[step],
            send_sem=near_ss.at[step],
            recv_sem=near_rs.at[step],
            device_id=near_peer(step),
            device_id_type=MESH,
        )
        for step in range(1, 8)
    ]
    for hop in hops:
        hop.start()
    joined = line[0]
    rows_load.wait()
    for step, hop in enumerate(hops):
        hop.wait_recv()
        joined = joined + near[step + 1]
    line[1] = joined
    leaps = [
        pltpu.make_async_remote_copy(
            src_ref=line.at[1],
            dst_ref=far.at[step],
            send_sem=far_ss.at[step],
            recv_sem=far_rs.at[step],
            device_id=far_peer(step),
            device_id_type=MESH,
        )
        for step in range(1, 16)
    ]
    for leap in leaps:
        leap.start()

    def product(step, values):
        owner = lax.rem(cell + 16 - step, 16)
        columns = pl.ds(pl.multiple_of(lax.div(owner, 2) * 128, 128), 128)
        return rows_r[:, columns] * values

    answer = product(0, joined)
    for message in first + second + third:
        message.wait_send()
    for hop in hops:
        hop.wait_send()
    for step, leap in enumerate(leaps):
        leap.wait_recv()
        answer = answer + product(step + 1, far[step + 1])
    coarse[...] = jnp.broadcast_to(jnp.sum(answer, axis=1, keepdims=True), (8, 128))
    for leap in leaps:
        leap.wait_send()


def shards(
    deformation_vector,
    heating_traction,
    heat_level,
    substance_label,
    substance_stiffness_list,
    subregion_spans,
    projection_basis,
    reduced_system_reciprocal,
):
    hbm = pl.BlockSpec(memory_space=pltpu.HBM)
    vmem = pl.BlockSpec(memory_space=pltpu.VMEM)
    smem = pl.BlockSpec(memory_space=pltpu.SMEM)
    field = pltpu.VMEM((3, NX + 2, 2, ROWS, 128), F32)
    scalar = pltpu.VMEM((NX, NY, 256), F32)
    dma = pltpu.SemaphoreType.DMA
    moved, residual, coarse = pl.pallas_call(
        kernel,
        out_shape=(
            jax.ShapeDtypeStruct((3, NX, NY, 256), F32),
            jax.ShapeDtypeStruct((3, NX, NY, 256), F32),
            jax.ShapeDtypeStruct((8, 128), F32),
        ),
        in_specs=[hbm, hbm, hbm, hbm, smem, smem, hbm, hbm],
        out_specs=(vmem, vmem, vmem),
        scratch_shapes=[
            field,
            field,
            field,
            pltpu.VMEM((3, NX, NY, 256), F32),
            scalar,
            pltpu.VMEM((NX, NY, 256), jnp.int32),
            scalar,
            scalar,
            scalar,
            pltpu.VMEM((8, 3, NX, NY, 256), jnp.bfloat16),
            pltpu.VMEM((8, 1024), F32),
            pltpu.VMEM((3, 3, 2, NY, 128), F32),
            pltpu.VMEM((3, 2, 3, 2, NX, 128), F32),
            pltpu.VMEM((3, 2, 3, 2, NX, 128), F32),
            pltpu.VMEM((3, 4, 8, 128), F32),
            pltpu.VMEM((3, 4, 8, 128), F32),
            pltpu.VMEM((NY, 256), F32),
            pltpu.VMEM((2, 1, 128), F32),
            pltpu.VMEM((8, 1, 128), F32),
            pltpu.VMEM((16, 1, 128), F32),
            dma((7,)),
            dma((3, 2)),
            dma((3, 2)),
            dma((3, 2)),
            dma((3, 2)),
            dma((3, 4)),
            dma((3, 4)),
            dma((8,)),
            dma((8,)),
            dma((16,)),
            dma((16,)),
        ],
        compiler_params=pltpu.CompilerParams(
            collective_id=0, has_side_effects=True, vmem_limit_bytes=44 * 1024 * 1024
        ),
    )(
        deformation_vector,
        heating_traction,
        heat_level,
        substance_label,
        substance_stiffness_list,
        subregion_spans,
        projection_basis,
        reduced_system_reciprocal,
    )
    return moved, residual, coarse[:, 0]


def solution(mesh):
    placed = (
        P(None, "grp", "sub", None),
        P(None, "grp", "sub", None),
        P("grp", "sub", None),
        P("grp", "sub", None),
        P(),
        P("grp", "sub"),
        P(None, None, "grp", "sub", None),
        P(("grp", "sub"), None),
    )
    return jax.shard_map(
        shards,
        mesh=mesh,
        in_specs=placed,
        out_specs=(P(None, "grp", "sub", None), P(None, "grp", "sub", None), P(("grp", "sub"))),
        check_vma=False,
    )
```

```python
import functools

import jax
import jax.numpy as jnp
from jax import lax
from jax.experimental import pallas as pl
from jax.experimental.pallas import tpu as pltpu
from jax.sharding import PartitionSpec as P

SHIFT = 1.0
ROBIN = 1.0
OMEGA = 0.6
MESH = pl.DeviceIdType.MESH

NX = 32
NY = 32
ROWS = 48
FIRST = 8
BATCH = 8
F32 = jnp.float32


def each(op, *pairs):
    return [op(*parts) for parts in zip(*pairs)]


def add(left, right):
    return each(lambda p, q: p + q, left, right)


def sub(left, right):
    return each(lambda p, q: p - q, left, right)


def mul(left, right):
    return each(lambda p, q: p * q, left, right)


def scaled(factor, pair):
    return [factor * part for part in pair]


def block(field, slope, bend, forcing, mu, beta, x, yb):
    row = FIRST + 8 * yb

    def at(source, component, dx, dy):
        return [source[component, x + 1 + dx, half, pl.ds(row + dy, 8), :] for half in (0, 1)]

    def own(ref, *lead):
        return [ref[(*lead, x, pl.ds(8 * yb, 8), pl.ds(128 * half, 128))] for half in (0, 1)]

    shear, mixed = own(mu), own(beta)
    cross = []
    for c, other in ((0, 1), (1, 0)):
        turn = sub(
            sub(at(field, other, 1, 1), at(field, other, 1, -1)),
            sub(at(field, other, -1, 1), at(field, other, -1, -1)),
        )
        ends = ((1, 0), (-1, 0)) if c == 0 else ((0, 1), (0, -1))
        lift = sub(at(slope, 2, *ends[0]), at(slope, 2, *ends[1]))
        cross.append(add(scaled(0.25, turn), lift))
    cross.append(
        add(
            sub(at(slope, 0, 1, 0), at(slope, 0, -1, 0)),
            sub(at(slope, 1, 0, 1), at(slope, 1, 0, -1)),
        )
    )
    centres, defects = [], []
    for c in range(3):
        centre = at(field, c, 0, 0)
        across = add(at(field, c, 1, 0), at(field, c, -1, 0))
        along = add(at(field, c, 0, 1), at(field, c, 0, -1))
        rest = own(bend, c)
        laplace = add(add(across, along), rest)
        second = (
            sub(across, scaled(2.0, centre)),
            sub(along, scaled(2.0, centre)),
            add(rest, scaled(4.0, centre)),
        )[c]
        graddiv = add(second, cross[c])
        force = own(forcing, c)
        defects.append(add(sub(force, centre), add(mul(shear, laplace), mul(mixed, graddiv))))
        centres.append(centre)
    return centres, defects, shear, mixed


def along_z(values, matrix):
    high = values.astype(jnp.bfloat16)
    low = (values - high.astype(F32)).astype(jnp.bfloat16)
    return jnp.dot(jnp.concatenate([high, low], axis=1), matrix, preferred_element_type=F32)


def kernel(
    deformation,
    traction,
    heat_level,
    label,
    stiffness,
    span,
    basis,
    reciprocal,
    moved,
    residual,
    coarse,
    v0,
    v1,
    v2,
    slope,
    bend,
    bands,
    fringe,
    table,
    force,
    heat,
    kind,
    beta,
    kappa,
    vectors,
    rows_r,
    rimmed,
    side_send,
    side_recv,
    corner_send,
    corner_recv,
    total,
    line,
    near,
    far,
    load_sem,
    face_ss,
    face_rs,
    side_ss,
    side_rs,
    corner_ss,
    corner_rs,
    near_ss,
    near_rs,
    far_ss,
    far_rs,
):
    grp = lax.axis_index("grp")
    sub_at = lax.axis_index("sub")
    place = lax.rem(sub_at, 8)
    column = lax.div(sub_at, 8)
    cell = grp * 4 + column

    mu = heat

    loads = [
        pltpu.make_async_copy(
            deformation.at[:, :, :, pl.ds(128 * half, 128)],
            v0.at[:, pl.ds(1, NX), half, pl.ds(FIRST, NY), :],
            load_sem.at[half],
        )
        for half in (0, 1)
    ]
    heat_load = pltpu.make_async_copy(heat_level, heat, load_sem.at[2])
    kind_load = pltpu.make_async_copy(label, kind, load_sem.at[3])
    force_load = pltpu.make_async_copy(traction, force, load_sem.at[4])
    rows_load = pltpu.make_async_copy(reciprocal, rows_r, load_sem.at[5])
    basis_load = pltpu.make_async_copy(basis, vectors, load_sem.at[6])
    for load in loads:
        load.start()
    table_load = pltpu.make_async_copy(stiffness, table, load_sem.at[7])
    table_load.start()
    heat_load.start()
    kind_load.start()
    force_load.start()

    def shifted(dx, dy):
        return (lax.rem(grp + 4 + dx, 4), lax.rem(sub_at + 32 + dy, 32))

    def near_peer(step):
        return (grp, column * 8 + lax.rem(place + step, 8))

    def far_peer(step):
        other = lax.rem(cell + step, 16)
        return (lax.div(other, 4), lax.rem(other, 4) * 8 + place)

    corners = ((-1, -1), (-1, 1), (1, -1), (1, 1))
    barrier = pltpu.get_barrier_semaphore()
    partners = [shifted(-1, 0), shifted(1, 0), shifted(0, -1), shifted(0, 1)]
    partners += [shifted(*corner) for corner in corners]
    partners += [near_peer(step) for step in range(1, 8)]
    partners += [far_peer(step) for step in range(1, 16)]
    for partner in partners:
        pl.semaphore_signal(barrier, inc=1, device_id=partner, device_id_type=MESH)

    lane = lax.broadcasted_iota(jnp.int32, (8, 128), 1)
    reach = span[0, 0]
    active = [lane < reach, lane + 128 < reach]

    above_diagonal = lax.broadcasted_iota(jnp.int32, (256, 256), 0) - lax.broadcasted_iota(jnp.int32, (256, 256), 1)
    beside = jnp.where(jnp.abs(above_diagonal) == 1, 1.0, 0.0)
    for part in (pl.ds(0, 256), pl.ds(256, 256)):
        bands[part, 0:256] = jnp.where(above_diagonal == 0, -6.0, beside).astype(jnp.bfloat16)
        bands[part, 256:512] = (0.25 * beside * above_diagonal.astype(F32)).astype(jnp.bfloat16)

    def derive(field):
        rows = pl.ds(FIRST, NY)

        @pl.loop(0, NX // BATCH)
        def _(batch):
            at = [(c, BATCH * batch + number) for number in range(BATCH) for c in range(3)]
            values = [
                jnp.concatenate([field[c, x + 1, half, rows, :] for half in (0, 1)], axis=1) for c, x in at
            ]
            found = along_z(jnp.concatenate(values, axis=0), bands[...])
            for number, (c, x) in enumerate(at):
                part = found[NY * number : NY * (number + 1)]
                bend[c, x] = part[:, 0:256]
                for half in (0, 1):
                    slope[c, x + 1, half, rows, :] = part[:, 256 + 128 * half : 384 + 128 * half]

    def messages(round_at, field, low_face, high_face):
        found = []
        for side, dx in enumerate((-1, 1)):
            source = (low_face, high_face)[side]
            found.append(
                pltpu.make_async_remote_copy(
                    src_ref=source,
                    dst_ref=field.at[:, 33 if dx < 0 else 0, :, pl.ds(FIRST, NY), :],
                    send_sem=face_ss.at[round_at, side],
                    recv_sem=face_rs.at[round_at, side],
                    device_id=shifted(dx, 0),
                    device_id_type=MESH,
                )
            )
        for side, dy in enumerate((-1, 1)):
            found.append(
                pltpu.make_async_remote_copy(
                    src_ref=side_send.at[round_at, side],
                    dst_ref=side_recv.at[round_at, 1 - side],
                    send_sem=side_ss.at[round_at, side],
                    recv_sem=side_rs.at[round_at, side],
                    device_id=shifted(0, dy),
                    device_id_type=MESH,
                )
            )
        for number, corner in enumerate(corners):
            found.append(
                pltpu.make_async_remote_copy(
                    src_ref=corner_send.at[round_at, number],
                    dst_ref=corner_recv.at[round_at, 3 - number],
                    send_sem=corner_ss.at[round_at, number],
                    recv_sem=corner_rs.at[round_at, number],
                    device_id=shifted(*corner),
                    device_id_type=MESH,
                )
            )
        return found

    inside = [
        jnp.where(flag, 1.0, 0.0).astype(F32) for flag in (grp > 0, grp < 3, sub_at > 0, sub_at < 31)
    ]

    def pack_corners(round_at, take):
        for number, (dx, dy) in enumerate(corners):
            for c in range(3):
                for half in (0, 1):
                    corner_send[round_at, number, pl.ds(2 * c + half, 1), :] = take(dx, dy, c, half)

    def unpack(round_at, field):
        for c in range(3):
            for half in (0, 1):
                for number, (dx, dy) in enumerate(corners):
                    keep = inside[0 if dx < 0 else 1] * inside[2 if dy < 0 else 3]
                    field[c, 0 if dx < 0 else 33, half, pl.ds(7 if dy < 0 else 40, 1), :] = (
                        corner_recv[round_at, number, pl.ds(2 * c + half, 1), :] * keep
                    )

        for side in (0, 1):

            @pl.when(grp == (0 if side == 0 else 3))
            def _():
                field[:, 0 if side == 0 else 33, :, pl.ds(FIRST, NY), :] = jnp.zeros((3, 2, NY, 128), F32)

        rows = pl.ds(FIRST, NY)
        values = [
            jnp.concatenate([field[c, plane, half, rows, :] for half in (0, 1)], axis=1)
            for plane in (0, 33)
            for c in (0, 2)
        ]
        values += [
            jnp.concatenate([side_recv[round_at, side, c, half] for half in (0, 1)], axis=1)
            for side in (0, 1)
            for c in (1, 2)
        ]
        found = along_z(jnp.concatenate(values, axis=0), bands[:, 256:512])
        number = 0
        for plane in (0, 33):
            for c in (0, 2):
                for half in (0, 1):
                    slope[c, plane, half, rows, :] = found[NY * number : NY * (number + 1), 128 * half : 128 * half + 128]
                number += 1
        for side in (0, 1):
            for c in (1, 2):
                for half in (0, 1):
                    fringe[side, c - 1, half] = found[NY * number : NY * (number + 1), 128 * half : 128 * half + 128]
                number += 1

        @pl.loop(0, NX)
        def _(x):
            for side in (0, 1):
                row = pl.ds(7 if side == 0 else 40, 1)
                for half in (0, 1):
                    for c in range(3):
                        field[c, x + 1, half, row, :] = (
                            side_recv[round_at, side, c, half, pl.ds(x, 1), :] * inside[2 + side]
                        )
                    for c in (1, 2):
                        slope[c, x + 1, half, row, :] = (
                            fringe[side, c - 1, half, pl.ds(x, 1), :] * inside[2 + side]
                        )

    def pack_side(round_at, field, x):
        for side in (0, 1):
            for c in range(3):
                for half in (0, 1):
                    side_send[round_at, side, c, half, pl.ds(x, 1), :] = field[
                        c, x + 1, half, pl.ds(FIRST if side == 0 else FIRST + NY - 1, 1), :
                    ]

    def field_corner(field):
        return lambda dx, dy, c, half: field[
            c, 1 if dx < 0 else NX, half, pl.ds(FIRST if dy < 0 else FIRST + NY - 1, 1), :
        ]

    def faces(field):
        return (
            field.at[:, 1, :, pl.ds(FIRST, NY), :],
            field.at[:, NX, :, pl.ds(FIRST, NY), :],
        )

    for load in loads:
        load.wait()
    basis_load.start()
    rows_load.start()

    @pl.loop(0, NX)
    def _(x):
        for c in range(3):
            for half in (0, 1):
                for yb in range(4):
                    rows = pl.ds(FIRST + 8 * yb, 8)
                    v0[c, x + 1, half, rows, :] = jnp.where(active[half], v0[c, x + 1, half, rows, :], 0.0)
        pack_side(0, v0, x)

    pack_corners(0, field_corner(v0))
    pl.semaphore_wait(barrier, len(partners))
    first = messages(0, v0, *faces(v0))
    for message in first:
        message.start()

    derive(v0)

    table_load.wait()
    heat_load.wait()
    kind_load.wait()
    force_load.wait()

    @pl.loop(0, NX)
    def _(x):
        for yb in range(4):
            for half in (0, 1):
                at = (x, pl.ds(8 * yb, 8), pl.ds(128 * half, 128))
                material = kind[at]
                shear = jnp.full((8, 128), table[0, 0], F32)
                lame = jnp.full((8, 128), table[1, 0], F32)
                for number in range(1, 4):
                    chosen = material == number
                    shear = jnp.where(chosen, table[0, number], shear)
                    lame = jnp.where(chosen, table[1, number], lame)
                weakening = jnp.where(active[half], 2.0 - heat[at], 0.0)
                shear = shear * weakening
                mixed = lame * weakening + shear
                mu[at] = shear
                beta[at] = mixed
                kappa[at] = OMEGA / (SHIFT + 6.0 * shear + 2.0 * mixed)
                for c in range(3):
                    force[(c,) + at] = jnp.where(active[half], force[(c,) + at], 0.0)

    for message in first:
        message.wait_recv()
    unpack(0, v0)

    def sweep_block(source, target, x, yb, also_out):
        centre, defects, shear, mixed = block(source, slope, bend, force, mu, beta, x, yb)
        step = [kappa[x, pl.ds(8 * yb, 8), pl.ds(128 * half, 128)] for half in (0, 1)]
        for c in range(3):
            new = add(centre[c], mul(step, defects[c]))
            for half in (0, 1):
                target[c, x + 1, half, pl.ds(FIRST + 8 * yb, 8), :] = new[half]
                if also_out:
                    moved[c, x, pl.ds(8 * yb, 8), pl.ds(128 * half, 128)] = new[half]
        return centre, defects, shear, mixed

    def first_edge(x, yb):
        slot = jnp.where(x == 0, 0, jnp.where(x == NX - 1, 1, 2))
        centre, defects, shear, mixed = sweep_block(v0, v1, x, yb, False)
        step = each(lambda p, q: OMEGA / (SHIFT + ROBIN + 6.0 * p + 2.0 * q), shear, mixed)
        for c in range(3):
            new = add(centre[c], mul(step, defects[c]))
            for half in (0, 1):
                rimmed[slot, c, half, pl.ds(8 * yb, 8), :] = new[half]

    @pl.loop(0, 2)
    def _(end):
        for yb in (1, 2):
            first_edge(end * (NX - 1), yb)

    @pl.loop(0, NX)
    def _(x):
        slot = jnp.where(x == 0, 0, jnp.where(x == NX - 1, 1, 2))
        for yb in (0, 3):
            first_edge(x, yb)
        for side in (0, 1):
            for c in range(3):
                for half in (0, 1):
                    side_send[1, side, c, half, pl.ds(x, 1), :] = rimmed[
                        slot, c, half, pl.ds(0 if side == 0 else NY - 1, 1), :
                    ]

    pack_corners(
        1,
        lambda dx, dy, c, half: rimmed[
            0 if dx < 0 else 1, c, half, pl.ds(0 if dy < 0 else NY - 1, 1), :
        ],
    )
    second = messages(1, v1, rimmed.at[0], rimmed.at[1])
    for message in second:
        message.start()

    @pl.loop(1, NX - 1)
    def _(x):
        for yb in (1, 2):
            sweep_block(v0, v1, x, yb, False)

    derive(v1)

    @pl.loop(1, NX - 1)
    def _(x):
        for yb in (1, 2):
            sweep_block(v1, v2, x, yb, True)

    for message in second:
        message.wait_recv()
    unpack(1, v1)

    @pl.loop(0, 2)
    def _(end):
        for yb in (1, 2):
            sweep_block(v1, v2, end * (NX - 1), yb, True)

    @pl.loop(0, NX)
    def _(x):
        for yb in (0, 3):
            sweep_block(v1, v2, x, yb, True)
        pack_side(2, v2, x)

    pack_corners(2, field_corner(v2))
    third = messages(2, v2, *faces(v2))
    for message in third:
        message.start()

    derive(v2)

    basis_load.wait()
    total[...] = jnp.zeros_like(total)

    def residual_block(x, yb):
        _, defects, _, _ = block(v2, slope, bend, force, mu, beta, x, yb)
        sums = [None] * 8
        pair = pl.ds(16 * (yb // 2), 16)
        upper = 8 * (yb % 2)
        for c in range(3):
            for half in (0, 1):
                columns = pl.ds(128 * half, 128)
                value = defects[c][half]
                residual[c, x, pl.ds(8 * yb, 8), columns] = value
                value = value.astype(jnp.bfloat16).astype(F32)
                for k in range(8):
                    vector = vectors[k, c, x, pair, columns].astype(F32)[upper : upper + 8]
                    term = vector * value
                    sums[k] = term if sums[k] is None else sums[k] + term
        return sums

    def gather_sums(found):
        for k in range(8):
            part = found[0][k]
            for other in found[1:]:
                part = part + other[k]
            total[k] += part

    @pl.loop(1, NX - 1)
    def _(x):
        gather_sums([residual_block(x, yb) for yb in (1, 2)])

    for message in third:
        message.wait_recv()
    unpack(2, v2)

    @pl.loop(0, 2)
    def _(end):
        gather_sums([residual_block(end * (NX - 1), yb) for yb in (1, 2)])

    @pl.loop(0, NX)
    def _(x):
        gather_sums([residual_block(x, yb) for yb in (0, 3)])

    start_lane = 64 * lax.rem(cell, 2) + 8 * place
    spread = jnp.zeros((8, 128), F32)
    for k in range(8):
        spread = jnp.where(lane == start_lane + k, jnp.sum(total[k], axis=1, keepdims=True), spread)
    line[0] = jnp.sum(spread, axis=0, keepdims=True)

    hops = [
        pltpu.make_async_remote_copy(
            src_ref=line.at[0],
            dst_ref=near.at[step],
            send_sem=near_ss.at[step],
            recv_sem=near_rs.at[step],
            device_id=near_peer(step),
            device_id_type=MESH,
        )
        for step in range(1, 8)
    ]
    for hop in hops:
        hop.start()
    joined = line[0]
    rows_load.wait()
    for step, hop in enumerate(hops):
        hop.wait_recv()
        joined = joined + near[step + 1]
    line[1] = joined
    leaps = [
        pltpu.make_async_remote_copy(
            src_ref=line.at[1],
            dst_ref=far.at[step],
            send_sem=far_ss.at[step],
            recv_sem=far_rs.at[step],
            device_id=far_peer(step),
            device_id_type=MESH,
        )
        for step in range(1, 16)
    ]
    for leap in leaps:
        leap.start()

    def product(step, values):
        owner = lax.rem(cell + 16 - step, 16)
        columns = pl.ds(pl.multiple_of(lax.div(owner, 2) * 128, 128), 128)
        return rows_r[:, columns] * values

    answer = product(0, joined)
    for message in first + second + third:
        message.wait_send()
    for hop in hops:
        hop.wait_send()
    for step, leap in enumerate(leaps):
        leap.wait_recv()
        answer = answer + product(step + 1, far[step + 1])
    coarse[...] = jnp.broadcast_to(jnp.sum(answer, axis=1, keepdims=True), (8, 128))
    for leap in leaps:
        leap.wait_send()


def shards(
    deformation_vector,
    heating_traction,
    heat_level,
    substance_label,
    substance_stiffness_list,
    subregion_spans,
    projection_basis,
    reduced_system_reciprocal,
):
    hbm = pl.BlockSpec(memory_space=pltpu.HBM)
    vmem = pl.BlockSpec(memory_space=pltpu.VMEM)
    smem = pl.BlockSpec(memory_space=pltpu.SMEM)
    field = pltpu.VMEM((3, NX + 2, 2, ROWS, 128), F32)
    scalar = pltpu.VMEM((NX, NY, 256), F32)
    dma = pltpu.SemaphoreType.DMA

    def far(array):
        return pltpu.with_memory_space_constraint(array, pltpu.HBM)

    moved, residual, coarse = pl.pallas_call(
        kernel,
        out_shape=(
            jax.ShapeDtypeStruct((3, NX, NY, 256), F32),
            jax.ShapeDtypeStruct((3, NX, NY, 256), F32),
            jax.ShapeDtypeStruct((8, 128), F32),
        ),
        in_specs=[hbm, hbm, hbm, hbm, hbm, smem, hbm, hbm],
        out_specs=(vmem, vmem, vmem),
        scratch_shapes=[
            field,
            field,
            field,
            field,
            pltpu.VMEM((3, NX, NY, 256), F32),
            pltpu.VMEM((512, 512), jnp.bfloat16),
            pltpu.VMEM((2, 2, 2, NX, 128), F32),
            pltpu.SMEM((2, 4), F32),
            pltpu.VMEM((3, NX, NY, 256), F32),
            scalar,
            pltpu.VMEM((NX, NY, 256), jnp.int32),
            scalar,
            scalar,
            pltpu.VMEM((8, 3, NX, NY, 256), jnp.bfloat16),
            pltpu.VMEM((8, 1024), F32),
            pltpu.VMEM((3, 3, 2, NY, 128), F32),
            pltpu.VMEM((3, 2, 3, 2, NX, 128), F32),
            pltpu.VMEM((3, 2, 3, 2, NX, 128), F32),
            pltpu.VMEM((3, 4, 8, 128), F32),
            pltpu.VMEM((3, 4, 8, 128), F32),
            pltpu.VMEM((8, 8, 128), F32),
            pltpu.VMEM((2, 1, 128), F32),
            pltpu.VMEM((8, 1, 128), F32),
            pltpu.VMEM((16, 1, 128), F32),
            dma((8,)),
            dma((3, 2)),
            dma((3, 2)),
            dma((3, 2)),
            dma((3, 2)),
            dma((3, 4)),
            dma((3, 4)),
            dma((8,)),
            dma((8,)),
            dma((16,)),
            dma((16,)),
        ],
        compiler_params=pltpu.CompilerParams(
            collective_id=0, has_side_effects=True, vmem_limit_bytes=46 * 1024 * 1024
        ),
    )(
        far(deformation_vector),
        far(heating_traction),
        far(heat_level),
        far(substance_label),
        far(substance_stiffness_list.T),
        subregion_spans,
        far(projection_basis),
        far(reduced_system_reciprocal),
    )
    return moved, residual, coarse[:, 0]


def solution(mesh):
    placed = (
        P(None, "grp", "sub", None),
        P(None, "grp", "sub", None),
        P("grp", "sub", None),
        P("grp", "sub", None),
        P(),
        P("grp", "sub"),
        P(None, None, "grp", "sub", None),
        P(("grp", "sub"), None),
    )
    return jax.shard_map(
        shards,
        mesh=mesh,
        in_specs=placed,
        out_specs=(P(None, "grp", "sub", None), P(None, "grp", "sub", None), P(("grp", "sub"))),
        check_vma=False,
    )
```

```python
import functools

import jax
import jax.numpy as jnp
from jax import lax
from jax.experimental import pallas as pl
from jax.experimental.pallas import tpu as pltpu
from jax.sharding import PartitionSpec as P

SHIFT = 1.0
ROBIN = 1.0
OMEGA = 0.6
MESH = pl.DeviceIdType.MESH

NX = 32
NY = 32
ROWS = 48
FIRST = 8
BATCH = 8
F32 = jnp.float32


def each(op, *pairs):
    return [op(*parts) for parts in zip(*pairs)]


def add(left, right):
    return each(lambda p, q: p + q, left, right)


def sub(left, right):
    return each(lambda p, q: p - q, left, right)


def mul(left, right):
    return each(lambda p, q: p * q, left, right)


def scaled(factor, pair):
    return [factor * part for part in pair]


def block(field, slope, bend, forcing, mu, beta, x, yb):
    row = FIRST + 8 * yb

    def at(source, component, dx, dy):
        return [source[component, x + 1 + dx, half, pl.ds(row + dy, 8), :] for half in (0, 1)]

    def own(ref, *lead):
        return [ref[(*lead, x, pl.ds(8 * yb, 8), pl.ds(128 * half, 128))] for half in (0, 1)]

    shear, mixed = own(mu), own(beta)
    cross = []
    for c, other in ((0, 1), (1, 0)):
        turn = sub(
            sub(at(field, other, 1, 1), at(field, other, 1, -1)),
            sub(at(field, other, -1, 1), at(field, other, -1, -1)),
        )
        ends = ((1, 0), (-1, 0)) if c == 0 else ((0, 1), (0, -1))
        lift = sub(at(slope, 2, *ends[0]), at(slope, 2, *ends[1]))
        cross.append(add(scaled(0.25, turn), lift))
    cross.append(
        add(
            sub(at(slope, 0, 1, 0), at(slope, 0, -1, 0)),
            sub(at(slope, 1, 0, 1), at(slope, 1, 0, -1)),
        )
    )
    centres, defects = [], []
    for c in range(3):
        centre = at(field, c, 0, 0)
        across = add(at(field, c, 1, 0), at(field, c, -1, 0))
        along = add(at(field, c, 0, 1), at(field, c, 0, -1))
        rest = own(bend, c)
        laplace = add(add(across, along), rest)
        second = (
            sub(across, scaled(2.0, centre)),
            sub(along, scaled(2.0, centre)),
            add(rest, scaled(4.0, centre)),
        )[c]
        graddiv = add(second, cross[c])
        force = own(forcing, c)
        defects.append(add(sub(force, centre), add(mul(shear, laplace), mul(mixed, graddiv))))
        centres.append(centre)
    return centres, defects, shear, mixed


def along_z(values, matrix):
    high = values.astype(jnp.bfloat16)
    low = (values - high.astype(F32)).astype(jnp.bfloat16)
    return jnp.dot(jnp.concatenate([high, low], axis=1), matrix, preferred_element_type=F32)


def kernel(
    deformation,
    traction,
    heat_level,
    label,
    stiffness,
    span,
    basis,
    reciprocal,
    moved,
    residual,
    coarse,
    v0,
    v1,
    v2,
    slope,
    bend,
    bands,
    fringe,
    table,
    force,
    heat,
    kind,
    beta,
    kappa,
    vectors,
    rows_r,
    rimmed,
    side_send,
    side_recv,
    corner_send,
    corner_recv,
    total,
    line,
    near,
    far,
    load_sem,
    face_ss,
    face_rs,
    side_ss,
    side_rs,
    corner_ss,
    corner_rs,
    near_ss,
    near_rs,
    far_ss,
    far_rs,
):
    grp = lax.axis_index("grp")
    sub_at = lax.axis_index("sub")
    place = lax.rem(sub_at, 8)
    column = lax.div(sub_at, 8)
    cell = grp * 4 + column

    mu = heat

    loads = [
        pltpu.make_async_copy(
            deformation.at[:, :, :, pl.ds(128 * half, 128)],
            v0.at[:, pl.ds(1, NX), half, pl.ds(FIRST, NY), :],
            load_sem.at[half],
        )
        for half in (0, 1)
    ]
    heat_load = pltpu.make_async_copy(heat_level, heat, load_sem.at[2])
    kind_load = pltpu.make_async_copy(label, kind, load_sem.at[3])
    force_load = pltpu.make_async_copy(traction, force, load_sem.at[4])
    rows_load = pltpu.make_async_copy(reciprocal, rows_r, load_sem.at[5])
    basis_load = pltpu.make_async_copy(basis, vectors, load_sem.at[6])
    for load in loads:
        load.start()
    table_load = pltpu.make_async_copy(stiffness, table, load_sem.at[7])
    table_load.start()
    heat_load.start()
    kind_load.start()
    force_load.start()

    def shifted(dx, dy):
        return (lax.rem(grp + 4 + dx, 4), lax.rem(sub_at + 32 + dy, 32))

    def near_peer(step):
        return (grp, column * 8 + lax.rem(place + step, 8))

    def far_peer(step):
        other = lax.rem(cell + step, 16)
        return (lax.div(other, 4), lax.rem(other, 4) * 8 + place)

    corners = ((-1, -1), (-1, 1), (1, -1), (1, 1))
    barrier = pltpu.get_barrier_semaphore()
    partners = [shifted(-1, 0), shifted(1, 0), shifted(0, -1), shifted(0, 1)]
    partners += [shifted(*corner) for corner in corners]
    partners += [near_peer(step) for step in range(1, 8)]
    partners += [far_peer(step) for step in range(1, 16)]
    for partner in partners:
        pl.semaphore_signal(barrier, inc=1, device_id=partner, device_id_type=MESH)

    lane = lax.broadcasted_iota(jnp.int32, (8, 128), 1)
    reach = span[0, 0]
    active = [lane < reach, lane + 128 < reach]

    above_diagonal = lax.broadcasted_iota(jnp.int32, (256, 256), 0) - lax.broadcasted_iota(jnp.int32, (256, 256), 1)
    beside = jnp.where(jnp.abs(above_diagonal) == 1, 1.0, 0.0)
    for part in (pl.ds(0, 256), pl.ds(256, 256)):
        bands[part, 0:256] = jnp.where(above_diagonal == 0, -6.0, beside).astype(jnp.bfloat16)
        bands[part, 256:512] = (0.25 * beside * above_diagonal.astype(F32)).astype(jnp.bfloat16)

    def derive(field):
        rows = pl.ds(FIRST, NY)

        @pl.loop(0, NX // BATCH)
        def _(batch):
            at = [(c, BATCH * batch + number) for number in range(BATCH) for c in range(3)]
            values = [
                jnp.concatenate([field[c, x + 1, half, rows, :] for half in (0, 1)], axis=1) for c, x in at
            ]
            found = along_z(jnp.concatenate(values, axis=0), bands[...])
            for number, (c, x) in enumerate(at):
                part = found[NY * number : NY * (number + 1)]
                bend[c, x] = part[:, 0:256]
                for half in (0, 1):
                    slope[c, x + 1, half, rows, :] = part[:, 256 + 128 * half : 384 + 128 * half]

    def messages(round_at, field, low_face, high_face):
        found = []
        for side, dx in enumerate((-1, 1)):
            source = (low_face, high_face)[side]
            found.append(
                pltpu.make_async_remote_copy(
                    src_ref=source,
                    dst_ref=field.at[:, 33 if dx < 0 else 0, :, pl.ds(FIRST, NY), :],
                    send_sem=face_ss.at[round_at, side],
                    recv_sem=face_rs.at[round_at, side],
                    device_id=shifted(dx, 0),
                    device_id_type=MESH,
                )
            )
        for side, dy in enumerate((-1, 1)):
            found.append(
                pltpu.make_async_remote_copy(
                    src_ref=side_send.at[round_at, side],
                    dst_ref=side_recv.at[round_at, 1 - side],
                    send_sem=side_ss.at[round_at, side],
                    recv_sem=side_rs.at[round_at, side],
                    device_id=shifted(0, dy),
                    device_id_type=MESH,
                )
            )
        for number, corner in enumerate(corners):
            found.append(
                pltpu.make_async_remote_copy(
                    src_ref=corner_send.at[round_at, number],
                    dst_ref=corner_recv.at[round_at, 3 - number],
                    send_sem=corner_ss.at[round_at, number],
                    recv_sem=corner_rs.at[round_at, number],
                    device_id=shifted(*corner),
                    device_id_type=MESH,
                )
            )
        return found

    inside = [
        jnp.where(flag, 1.0, 0.0).astype(F32) for flag in (grp > 0, grp < 3, sub_at > 0, sub_at < 31)
    ]

    def pack_corners(round_at, take):
        for number, (dx, dy) in enumerate(corners):
            for c in range(3):
                for half in (0, 1):
                    corner_send[round_at, number, pl.ds(2 * c + half, 1), :] = take(dx, dy, c, half)

    def unpack_sides(round_at, field):
        values = [
            jnp.concatenate([side_recv[round_at, side, c, half] for half in (0, 1)], axis=1)
            for side in (0, 1)
            for c in (1, 2)
        ]
        found = along_z(jnp.concatenate(values, axis=0), bands[:, 256:512])
        number = 0
        for side in (0, 1):
            for c in (1, 2):
                for half in (0, 1):
                    fringe[side, c - 1, half] = found[NY * number : NY * (number + 1), 128 * half : 128 * half + 128]
                number += 1

        @pl.loop(0, NX // 2)
        def _(pair):
            for x in (2 * pair, 2 * pair + 1):
                for side in (0, 1):
                    row = pl.ds(7 if side == 0 else 40, 1)
                    for half in (0, 1):
                        for c in range(3):
                            field[c, x + 1, half, row, :] = (
                                side_recv[round_at, side, c, half, pl.ds(x, 1), :] * inside[2 + side]
                            )
                        for c in (1, 2):
                            slope[c, x + 1, half, row, :] = (
                                fringe[side, c - 1, half, pl.ds(x, 1), :] * inside[2 + side]
                            )

    def unpack_faces(round_at, field):
        for c in range(3):
            for half in (0, 1):
                for number, (dx, dy) in enumerate(corners):
                    keep = inside[0 if dx < 0 else 1] * inside[2 if dy < 0 else 3]
                    field[c, 0 if dx < 0 else 33, half, pl.ds(7 if dy < 0 else 40, 1), :] = (
                        corner_recv[round_at, number, pl.ds(2 * c + half, 1), :] * keep
                    )
        for side in (0, 1):

            @pl.when(grp == (0 if side == 0 else 3))
            def _():
                field[:, 0 if side == 0 else 33, :, pl.ds(FIRST, NY), :] = jnp.zeros((3, 2, NY, 128), F32)

        rows = pl.ds(FIRST, NY)
        values = [
            jnp.concatenate([field[c, plane, half, rows, :] for half in (0, 1)], axis=1)
            for plane in (0, 33)
            for c in (0, 2)
        ]
        found = along_z(jnp.concatenate(values, axis=0), bands[:, 256:512])
        number = 0
        for plane in (0, 33):
            for c in (0, 2):
                for half in (0, 1):
                    slope[c, plane, half, rows, :] = found[NY * number : NY * (number + 1), 128 * half : 128 * half + 128]
                number += 1

    def edges(round_at, found, field, work):
        for message in found[2:4]:
            message.wait_recv()
        unpack_sides(round_at, field)

        @pl.loop(0, NX // 2 - 1)
        def _(pair):
            work(2 * pair + 1, (0, 3))
            work(2 * pair + 2, (0, 3))

        for message in found[0:2] + found[4:8]:
            message.wait_recv()
        unpack_faces(round_at, field)

        @pl.loop(0, 2)
        def _(end):
            work(end * (NX - 1), (0, 1, 2, 3))

    def interior(work):
        @pl.loop(0, NX // 2 - 1)
        def _(pair):
            work(2 * pair + 1, (1, 2))
            work(2 * pair + 2, (1, 2))

    def pack_side(round_at, field, x):
        for side in (0, 1):
            for c in range(3):
                for half in (0, 1):
                    side_send[round_at, side, c, half, pl.ds(x, 1), :] = field[
                        c, x + 1, half, pl.ds(FIRST if side == 0 else FIRST + NY - 1, 1), :
                    ]

    def field_corner(field):
        return lambda dx, dy, c, half: field[
            c, 1 if dx < 0 else NX, half, pl.ds(FIRST if dy < 0 else FIRST + NY - 1, 1), :
        ]

    def faces(field):
        return (
            field.at[:, 1, :, pl.ds(FIRST, NY), :],
            field.at[:, NX, :, pl.ds(FIRST, NY), :],
        )

    for load in loads:
        load.wait()
    basis_load.start()
    rows_load.start()

    @pl.loop(0, NX)
    def _(x):
        for c in range(3):
            for half in (0, 1):
                for yb in range(4):
                    rows = pl.ds(FIRST + 8 * yb, 8)
                    v0[c, x + 1, half, rows, :] = jnp.where(active[half], v0[c, x + 1, half, rows, :], 0.0)
        pack_side(0, v0, x)

    pl.semaphore_wait(barrier, len(partners))
    first = messages(0, v0, *faces(v0))
    for message in first[:4]:
        message.start()
    pack_corners(0, field_corner(v0))
    for message in first[4:]:
        message.start()

    derive(v0)

    table_load.wait()
    heat_load.wait()
    kind_load.wait()
    force_load.wait()

    @pl.loop(0, NX)
    def _(x):
        for yb in range(4):
            for half in (0, 1):
                at = (x, pl.ds(8 * yb, 8), pl.ds(128 * half, 128))
                material = kind[at]
                shear = jnp.full((8, 128), table[0, 0], F32)
                lame = jnp.full((8, 128), table[1, 0], F32)
                for number in range(1, 4):
                    chosen = material == number
                    shear = jnp.where(chosen, table[0, number], shear)
                    lame = jnp.where(chosen, table[1, number], lame)
                weakening = jnp.where(active[half], 2.0 - heat[at], 0.0)
                shear = shear * weakening
                mixed = lame * weakening + shear
                mu[at] = shear
                beta[at] = mixed
                kappa[at] = OMEGA / (SHIFT + 6.0 * shear + 2.0 * mixed)
                for c in range(3):
                    force[(c,) + at] = jnp.where(active[half], force[(c,) + at], 0.0)

    def sweep_block(source, target, x, yb, also_out):
        centre, defects, shear, mixed = block(source, slope, bend, force, mu, beta, x, yb)
        step = [kappa[x, pl.ds(8 * yb, 8), pl.ds(128 * half, 128)] for half in (0, 1)]
        for c in range(3):
            new = add(centre[c], mul(step, defects[c]))
            for half in (0, 1):
                target[c, x + 1, half, pl.ds(FIRST + 8 * yb, 8), :] = new[half]
                if also_out:
                    moved[c, x, pl.ds(8 * yb, 8), pl.ds(128 * half, 128)] = new[half]
        return centre, defects, shear, mixed

    def first_edge(x, blocks):
        slot = jnp.where(x == 0, 0, jnp.where(x == NX - 1, 1, 2))
        for yb in blocks:
            centre, defects, shear, mixed = sweep_block(v0, v1, x, yb, False)
            step = each(lambda p, q: OMEGA / (SHIFT + ROBIN + 6.0 * p + 2.0 * q), shear, mixed)
            for c in range(3):
                new = add(centre[c], mul(step, defects[c]))
                for half in (0, 1):
                    rimmed[slot, c, half, pl.ds(8 * yb, 8), :] = new[half]
        for side in (0, 1):
            for c in range(3):
                for half in (0, 1):
                    side_send[1, side, c, half, pl.ds(x, 1), :] = rimmed[
                        slot, c, half, pl.ds(0 if side == 0 else NY - 1, 1), :
                    ]

    def first_rest(x, blocks):
        for yb in blocks:
            sweep_block(v0, v1, x, yb, False)

    def second_rest(x, blocks):
        for yb in blocks:
            sweep_block(v1, v2, x, yb, True)

    def second_edge(x, blocks):
        second_rest(x, blocks)
        pack_side(2, v2, x)

    edges(0, first, v0, first_edge)
    second = messages(1, v1, rimmed.at[0], rimmed.at[1])
    for message in second[:4]:
        message.start()
    pack_corners(
        1,
        lambda dx, dy, c, half: rimmed[
            0 if dx < 0 else 1, c, half, pl.ds(0 if dy < 0 else NY - 1, 1), :
        ],
    )
    for message in second[4:]:
        message.start()

    interior(first_rest)
    derive(v1)
    interior(second_rest)
    edges(1, second, v1, second_edge)
    third = messages(2, v2, *faces(v2))
    for message in third[:4]:
        message.start()
    pack_corners(2, field_corner(v2))
    for message in third[4:]:
        message.start()
    derive(v2)

    basis_load.wait()
    total[...] = jnp.zeros_like(total)

    def residual_block(x, yb):
        _, defects, _, _ = block(v2, slope, bend, force, mu, beta, x, yb)
        sums = [None] * 8
        pair = pl.ds(16 * (yb // 2), 16)
        upper = 8 * (yb % 2)
        for c in range(3):
            for half in (0, 1):
                columns = pl.ds(128 * half, 128)
                value = defects[c][half]
                residual[c, x, pl.ds(8 * yb, 8), columns] = value
                value = value.astype(jnp.bfloat16).astype(F32)
                for k in range(8):
                    vector = vectors[k, c, x, pair, columns].astype(F32)[upper : upper + 8]
                    term = vector * value
                    sums[k] = term if sums[k] is None else sums[k] + term
        return sums

    def gather_sums(found):
        for k in range(8):
            part = found[0][k]
            for other in found[1:]:
                part = part + other[k]
            total[k] += part

    def residual_work(x, blocks):
        gather_sums([residual_block(x, yb) for yb in blocks])

    interior(residual_work)
    edges(2, third, v2, residual_work)

    start_lane = 64 * lax.rem(cell, 2) + 8 * place
    spread = jnp.zeros((8, 128), F32)
    for k in range(8):
        spread = jnp.where(lane == start_lane + k, jnp.sum(total[k], axis=1, keepdims=True), spread)
    line[0] = jnp.sum(spread, axis=0, keepdims=True)

    hops = [
        pltpu.make_async_remote_copy(
            src_ref=line.at[0],
            dst_ref=near.at[step],
            send_sem=near_ss.at[step],
            recv_sem=near_rs.at[step],
            device_id=near_peer(step),
            device_id_type=MESH,
        )
        for step in range(1, 8)
    ]
    for hop in hops:
        hop.start()
    joined = line[0]
    rows_load.wait()
    for step, hop in enumerate(hops):
        hop.wait_recv()
        joined = joined + near[step + 1]
    line[1] = joined
    leaps = [
        pltpu.make_async_remote_copy(
            src_ref=line.at[1],
            dst_ref=far.at[step],
            send_sem=far_ss.at[step],
            recv_sem=far_rs.at[step],
            device_id=far_peer(step),
            device_id_type=MESH,
        )
        for step in range(1, 16)
    ]
    for leap in leaps:
        leap.start()

    def product(step, values):
        owner = lax.rem(cell + 16 - step, 16)
        columns = pl.ds(pl.multiple_of(lax.div(owner, 2) * 128, 128), 128)
        return rows_r[:, columns] * values

    answer = product(0, joined)
    for message in first + second + third:
        message.wait_send()
    for hop in hops:
        hop.wait_send()
    for step, leap in enumerate(leaps):
        leap.wait_recv()
        answer = answer + product(step + 1, far[step + 1])
    own_lane = lane == lax.broadcasted_iota(jnp.int32, (8, 128), 0)
    coarse[...] = jnp.sum(
        jnp.where(own_lane, jnp.sum(answer, axis=1, keepdims=True), 0.0), axis=0, keepdims=True
    )
    for leap in leaps:
        leap.wait_send()


def finish(moved, residual, coarse, moved_out, residual_out, coarse_out, store_sem):
    stores = [
        pltpu.make_async_copy(source.at[c], target.at[c], store_sem.at[number, c])
        for number, (source, target) in enumerate(((moved, moved_out), (residual, residual_out)))
        for c in range(3)
    ]
    for store in stores:
        store.start()
    coarse_out[...] = coarse[0, 0:8]
    for store in stores:
        store.wait()


def shards(
    deformation_vector,
    heating_traction,
    heat_level,
    substance_label,
    substance_stiffness_list,
    subregion_spans,
    projection_basis,
    reduced_system_reciprocal,
):
    hbm = pl.BlockSpec(memory_space=pltpu.HBM)
    vmem = pl.BlockSpec(memory_space=pltpu.VMEM)
    smem = pl.BlockSpec(memory_space=pltpu.SMEM)
    field = pltpu.VMEM((3, NX + 2, 2, ROWS, 128), F32)
    scalar = pltpu.VMEM((NX, NY, 256), F32)
    dma = pltpu.SemaphoreType.DMA

    def far(array):
        return pltpu.with_memory_space_constraint(array, pltpu.HBM)

    moved, residual, coarse = pl.pallas_call(
        kernel,
        out_shape=(
            jax.ShapeDtypeStruct((3, NX, NY, 256), F32),
            jax.ShapeDtypeStruct((3, NX, NY, 256), F32),
            jax.ShapeDtypeStruct((1, 128), F32),
        ),
        in_specs=[hbm, hbm, hbm, hbm, hbm, smem, hbm, hbm],
        out_specs=(vmem, vmem, vmem),
        scratch_shapes=[
            field,
            field,
            field,
            field,
            pltpu.VMEM((3, NX, NY, 256), F32),
            pltpu.VMEM((512, 512), jnp.bfloat16),
            pltpu.VMEM((2, 2, 2, NX, 128), F32),
            pltpu.SMEM((2, 4), F32),
            pltpu.VMEM((3, NX, NY, 256), F32),
            scalar,
            pltpu.VMEM((NX, NY, 256), jnp.int32),
            scalar,
            scalar,
            pltpu.VMEM((8, 3, NX, NY, 256), jnp.bfloat16),
            pltpu.VMEM((8, 1024), F32),
            pltpu.VMEM((3, 3, 2, NY, 128), F32),
            pltpu.VMEM((3, 2, 3, 2, NX, 128), F32),
            pltpu.VMEM((3, 2, 3, 2, NX, 128), F32),
            pltpu.VMEM((3, 4, 8, 128), F32),
            pltpu.VMEM((3, 4, 8, 128), F32),
            pltpu.VMEM((8, 8, 128), F32),
            pltpu.VMEM((2, 1, 128), F32),
            pltpu.VMEM((8, 1, 128), F32),
            pltpu.VMEM((16, 1, 128), F32),
            dma((8,)),
            dma((3, 2)),
            dma((3, 2)),
            dma((3, 2)),
            dma((3, 2)),
            dma((3, 4)),
            dma((3, 4)),
            dma((8,)),
            dma((8,)),
            dma((16,)),
            dma((16,)),
        ],
        compiler_params=pltpu.CompilerParams(
            collective_id=0, has_side_effects=True, vmem_limit_bytes=46 * 1024 * 1024
        ),
    )(
        far(deformation_vector),
        far(heating_traction),
        far(heat_level),
        far(substance_label),
        far(substance_stiffness_list.T),
        subregion_spans,
        far(projection_basis),
        far(reduced_system_reciprocal),
    )
    return pl.pallas_call(
        finish,
        out_shape=(
            jax.ShapeDtypeStruct((3, NX, NY, 256), F32),
            jax.ShapeDtypeStruct((3, NX, NY, 256), F32),
            jax.ShapeDtypeStruct((8,), F32),
        ),
        in_specs=[vmem, vmem, vmem],
        out_specs=(hbm, hbm, vmem),
        scratch_shapes=[dma((2, 3))],
        compiler_params=pltpu.CompilerParams(vmem_limit_bytes=1024 * 1024),
    )(moved, residual, coarse)


def solution(mesh):
    placed = (
        P(None, "grp", "sub", None),
        P(None, "grp", "sub", None),
        P("grp", "sub", None),
        P("grp", "sub", None),
        P(),
        P("grp", "sub"),
        P(None, None, "grp", "sub", None),
        P(("grp", "sub"), None),
    )
    return jax.shard_map(
        shards,
        mesh=mesh,
        in_specs=placed,
        out_specs=(P(None, "grp", "sub", None), P(None, "grp", "sub", None), P(("grp", "sub"))),
        check_vma=False,
    )
```

```python
import functools

import jax
import jax.numpy as jnp
from jax import lax
from jax.experimental import pallas as pl
from jax.experimental.pallas import tpu as pltpu
from jax.sharding import PartitionSpec as P

SHIFT = 1.0
ROBIN = 1.0
OMEGA = 0.6
MESH = pl.DeviceIdType.MESH


def far_first(sizes):
    found = [(p, q) for p in range(sizes[0]) for q in range(sizes[1]) if p or q]
    return sorted(found, key=lambda at: (-sum(min(d, size - d) for d, size in zip(at, sizes)), at))


NEAR = far_first((4, 2))
FAR = far_first((4, 4))

NX = 32
NY = 32
ROWS = 48
FIRST = 8
BATCH = 8
F32 = jnp.float32


def each(op, *pairs):
    return [op(*parts) for parts in zip(*pairs)]


def add(left, right):
    return each(lambda p, q: p + q, left, right)


def sub(left, right):
    return each(lambda p, q: p - q, left, right)


def mul(left, right):
    return each(lambda p, q: p * q, left, right)


def scaled(factor, pair):
    return [factor * part for part in pair]


def block(field, slope, bend, forcing, mu, beta, x, yb):
    row = FIRST + 8 * yb

    def at(source, component, dx, dy):
        return [source[component, x + 1 + dx, half, pl.ds(row + dy, 8), :] for half in (0, 1)]

    def own(ref, *lead):
        return [ref[(*lead, x, pl.ds(8 * yb, 8), pl.ds(128 * half, 128))] for half in (0, 1)]

    shear, mixed = own(mu), own(beta)
    cross = []
    for c, other in ((0, 1), (1, 0)):
        turn = sub(
            sub(at(field, other, 1, 1), at(field, other, 1, -1)),
            sub(at(field, other, -1, 1), at(field, other, -1, -1)),
        )
        ends = ((1, 0), (-1, 0)) if c == 0 else ((0, 1), (0, -1))
        lift = sub(at(slope, 2, *ends[0]), at(slope, 2, *ends[1]))
        cross.append(add(scaled(0.25, turn), lift))
    cross.append(
        add(
            sub(at(slope, 0, 1, 0), at(slope, 0, -1, 0)),
            sub(at(slope, 1, 0, 1), at(slope, 1, 0, -1)),
        )
    )
    centres, defects = [], []
    for c in range(3):
        centre = at(field, c, 0, 0)
        across = add(at(field, c, 1, 0), at(field, c, -1, 0))
        along = add(at(field, c, 0, 1), at(field, c, 0, -1))
        rest = own(bend, c)
        laplace = add(add(across, along), rest)
        second = (
            sub(across, scaled(2.0, centre)),
            sub(along, scaled(2.0, centre)),
            add(rest, scaled(4.0, centre)),
        )[c]
        graddiv = add(second, cross[c])
        force = own(forcing, c)
        defects.append(add(sub(force, centre), add(mul(shear, laplace), mul(mixed, graddiv))))
        centres.append(centre)
    return centres, defects, shear, mixed


def along_z(values, matrix):
    high = values.astype(jnp.bfloat16)
    low = (values - high.astype(F32)).astype(jnp.bfloat16)
    return jnp.dot(jnp.concatenate([high, low], axis=1), matrix, preferred_element_type=F32)


def kernel(
    deformation,
    traction,
    heat_level,
    label,
    stiffness,
    span,
    basis,
    reciprocal,
    moved,
    residual,
    coarse,
    v0,
    v1,
    v2,
    slope,
    bend,
    bands,
    fringe,
    table,
    force,
    heat,
    kind,
    beta,
    kappa,
    vectors,
    rows_r,
    rimmed,
    side_send,
    side_recv,
    corner_send,
    corner_recv,
    total,
    line,
    near,
    far,
    load_sem,
    face_ss,
    face_rs,
    side_ss,
    side_rs,
    corner_ss,
    corner_rs,
    near_ss,
    near_rs,
    far_ss,
    far_rs,
):
    grp = lax.axis_index("grp")
    sub_at = lax.axis_index("sub")
    place = lax.rem(sub_at, 8)
    column = lax.div(sub_at, 8)
    cell = grp * 4 + column

    mu = heat

    loads = [
        pltpu.make_async_copy(
            deformation.at[:, :, :, pl.ds(128 * half, 128)],
            v0.at[:, pl.ds(1, NX), half, pl.ds(FIRST, NY), :],
            load_sem.at[half],
        )
        for half in (0, 1)
    ]
    heat_load = pltpu.make_async_copy(heat_level, heat, load_sem.at[2])
    kind_load = pltpu.make_async_copy(label, kind, load_sem.at[3])
    force_load = pltpu.make_async_copy(traction, force, load_sem.at[4])
    rows_load = pltpu.make_async_copy(reciprocal, rows_r, load_sem.at[5])
    basis_load = pltpu.make_async_copy(basis, vectors, load_sem.at[6])
    for load in loads:
        load.start()
    table_load = pltpu.make_async_copy(stiffness, table, load_sem.at[7])
    table_load.start()
    heat_load.start()
    kind_load.start()
    force_load.start()

    def shifted(dx, dy):
        return (lax.rem(grp + 4 + dx, 4), lax.rem(sub_at + 32 + dy, 32))

    def near_peer(step):
        dy, dc = NEAR[step]
        other = lax.rem(lax.div(place, 2) + dy, 4) * 2 + lax.rem(place + dc, 2)
        return (grp, column * 8 + other)

    def far_peer(step):
        dz, dx = FAR[step]
        return (lax.rem(grp + dz, 4), lax.rem(column + dx, 4) * 8 + place)

    corners = ((-1, -1), (-1, 1), (1, -1), (1, 1))
    barrier = pltpu.get_barrier_semaphore()
    partners = [shifted(-1, 0), shifted(1, 0), shifted(0, -1), shifted(0, 1)]
    partners += [shifted(*corner) for corner in corners]
    partners += [near_peer(step) for step in range(7)]
    partners += [far_peer(step) for step in range(15)]
    for partner in partners:
        pl.semaphore_signal(barrier, inc=1, device_id=partner, device_id_type=MESH)

    lane = lax.broadcasted_iota(jnp.int32, (8, 128), 1)
    reach = span[0, 0]
    active = [lane < reach, lane + 128 < reach]

    above_diagonal = lax.broadcasted_iota(jnp.int32, (256, 256), 0) - lax.broadcasted_iota(jnp.int32, (256, 256), 1)
    beside = jnp.where(jnp.abs(above_diagonal) == 1, 1.0, 0.0)
    for part in (pl.ds(0, 256), pl.ds(256, 256)):
        bands[part, 0:256] = jnp.where(above_diagonal == 0, -6.0, beside).astype(jnp.bfloat16)
        bands[part, 256:512] = (0.25 * beside * above_diagonal.astype(F32)).astype(jnp.bfloat16)

    def derive(field):
        rows = pl.ds(FIRST, NY)

        @pl.loop(0, NX // BATCH)
        def _(batch):
            at = [(c, BATCH * batch + number) for number in range(BATCH) for c in range(3)]
            values = [
                jnp.concatenate([field[c, x + 1, half, rows, :] for half in (0, 1)], axis=1) for c, x in at
            ]
            found = along_z(jnp.concatenate(values, axis=0), bands[...])
            for number, (c, x) in enumerate(at):
                part = found[NY * number : NY * (number + 1)]
                bend[c, x] = part[:, 0:256]
                for half in (0, 1):
                    slope[c, x + 1, half, rows, :] = part[:, 256 + 128 * half : 384 + 128 * half]

    def messages(round_at, field, low_face, high_face):
        found = []
        for side, dx in enumerate((-1, 1)):
            source = (low_face, high_face)[side]
            found.append(
                pltpu.make_async_remote_copy(
                    src_ref=source,
                    dst_ref=field.at[:, 33 if dx < 0 else 0, :, pl.ds(FIRST, NY), :],
                    send_sem=face_ss.at[round_at, side],
                    recv_sem=face_rs.at[round_at, side],
                    device_id=shifted(dx, 0),
                    device_id_type=MESH,
                )
            )
        for side, dy in enumerate((-1, 1)):
            found.append(
                pltpu.make_async_remote_copy(
                    src_ref=side_send.at[round_at, side],
                    dst_ref=side_recv.at[round_at, 1 - side],
                    send_sem=side_ss.at[round_at, side],
                    recv_sem=side_rs.at[round_at, side],
                    device_id=shifted(0, dy),
                    device_id_type=MESH,
                )
            )
        for number, corner in enumerate(corners):
            found.append(
                pltpu.make_async_remote_copy(
                    src_ref=corner_send.at[round_at, number],
                    dst_ref=corner_recv.at[round_at, 3 - number],
                    send_sem=corner_ss.at[round_at, number],
                    recv_sem=corner_rs.at[round_at, number],
                    device_id=shifted(*corner),
                    device_id_type=MESH,
                )
            )
        return found

    inside = [
        jnp.where(flag, 1.0, 0.0).astype(F32) for flag in (grp > 0, grp < 3, sub_at > 0, sub_at < 31)
    ]

    def pack_corners(round_at, take):
        for number, (dx, dy) in enumerate(corners):
            for c in range(3):
                for half in (0, 1):
                    corner_send[round_at, number, pl.ds(2 * c + half, 1), :] = take(dx, dy, c, half)

    def unpack_sides(round_at, field):
        values = [
            jnp.concatenate([side_recv[round_at, side, c, half] for half in (0, 1)], axis=1)
            for side in (0, 1)
            for c in (1, 2)
        ]
        found = along_z(jnp.concatenate(values, axis=0), bands[:, 256:512])
        number = 0
        for side in (0, 1):
            for c in (1, 2):
                for half in (0, 1):
                    fringe[side, c - 1, half] = found[NY * number : NY * (number + 1), 128 * half : 128 * half + 128]
                number += 1

    def unpack_rows(round_at, field, x):
        for side in (0, 1):
            row = pl.ds(7 if side == 0 else 40, 1)
            for half in (0, 1):
                for c in range(3):
                    field[c, x + 1, half, row, :] = (
                        side_recv[round_at, side, c, half, pl.ds(x, 1), :] * inside[2 + side]
                    )
                for c in (1, 2):
                    slope[c, x + 1, half, row, :] = (
                        fringe[side, c - 1, half, pl.ds(x, 1), :] * inside[2 + side]
                    )

    def unpack_faces(round_at, field):
        for c in range(3):
            for half in (0, 1):
                for number, (dx, dy) in enumerate(corners):
                    keep = inside[0 if dx < 0 else 1] * inside[2 if dy < 0 else 3]
                    field[c, 0 if dx < 0 else 33, half, pl.ds(7 if dy < 0 else 40, 1), :] = (
                        corner_recv[round_at, number, pl.ds(2 * c + half, 1), :] * keep
                    )
        for side in (0, 1):

            @pl.when(grp == (0 if side == 0 else 3))
            def _():
                field[:, 0 if side == 0 else 33, :, pl.ds(FIRST, NY), :] = jnp.zeros((3, 2, NY, 128), F32)

        rows = pl.ds(FIRST, NY)
        values = [
            jnp.concatenate([field[c, plane, half, rows, :] for half in (0, 1)], axis=1)
            for plane in (0, 33)
            for c in (0, 2)
        ]
        found = along_z(jnp.concatenate(values, axis=0), bands[:, 256:512])
        number = 0
        for plane in (0, 33):
            for c in (0, 2):
                for half in (0, 1):
                    slope[c, plane, half, rows, :] = found[NY * number : NY * (number + 1), 128 * half : 128 * half + 128]
                number += 1

    def edges(round_at, found, field, work):
        for message in found[2:4]:
            message.wait_recv()
        unpack_sides(round_at, field)
        unpack_rows(round_at, field, 0)
        unpack_rows(round_at, field, 1)

        @pl.loop(0, NX // 2 - 1)
        def _(pair):
            unpack_rows(round_at, field, 2 * pair + 2)
            unpack_rows(round_at, field, 2 * pair + 3)
            work(2 * pair + 1, (0, 3))
            work(2 * pair + 2, (0, 3))

        for message in found[0:2] + found[4:8]:
            message.wait_recv()
        unpack_faces(round_at, field)

        @pl.loop(0, 2)
        def _(end):
            work(end * (NX - 1), (0, 1, 2, 3))

    def interior(work):
        @pl.loop(0, NX // 2 - 1)
        def _(pair):
            work(2 * pair + 1, (1, 2))
            work(2 * pair + 2, (1, 2))

    def pack_side(round_at, field, x):
        for side in (0, 1):
            for c in range(3):
                for half in (0, 1):
                    side_send[round_at, side, c, half, pl.ds(x, 1), :] = field[
                        c, x + 1, half, pl.ds(FIRST if side == 0 else FIRST + NY - 1, 1), :
                    ]

    def field_corner(field):
        return lambda dx, dy, c, half: field[
            c, 1 if dx < 0 else NX, half, pl.ds(FIRST if dy < 0 else FIRST + NY - 1, 1), :
        ]

    def faces(field):
        return (
            field.at[:, 1, :, pl.ds(FIRST, NY), :],
            field.at[:, NX, :, pl.ds(FIRST, NY), :],
        )

    for load in loads:
        load.wait()
    basis_load.start()
    rows_load.start()

    @pl.loop(0, NX)
    def _(x):
        for c in range(3):
            for half in (0, 1):
                for yb in range(4):
                    rows = pl.ds(FIRST + 8 * yb, 8)
                    v0[c, x + 1, half, rows, :] = jnp.where(active[half], v0[c, x + 1, half, rows, :], 0.0)
        pack_side(0, v0, x)

    pl.semaphore_wait(barrier, len(partners))
    first = messages(0, v0, *faces(v0))
    for message in first[:4]:
        message.start()
    pack_corners(0, field_corner(v0))
    for message in first[4:]:
        message.start()

    derive(v0)

    table_load.wait()
    heat_load.wait()
    kind_load.wait()
    force_load.wait()

    @pl.loop(0, NX)
    def _(x):
        for yb in range(4):
            for half in (0, 1):
                at = (x, pl.ds(8 * yb, 8), pl.ds(128 * half, 128))
                material = kind[at]
                shear = jnp.full((8, 128), table[0, 0], F32)
                lame = jnp.full((8, 128), table[1, 0], F32)
                for number in range(1, 4):
                    chosen = material == number
                    shear = jnp.where(chosen, table[0, number], shear)
                    lame = jnp.where(chosen, table[1, number], lame)
                weakening = jnp.where(active[half], 2.0 - heat[at], 0.0)
                shear = shear * weakening
                mixed = lame * weakening + shear
                mu[at] = shear
                beta[at] = mixed
                kappa[at] = OMEGA / (SHIFT + 6.0 * shear + 2.0 * mixed)
                for c in range(3):
                    force[(c,) + at] = jnp.where(active[half], force[(c,) + at], 0.0)

    def sweep_block(source, target, x, yb, also_out):
        centre, defects, shear, mixed = block(source, slope, bend, force, mu, beta, x, yb)
        step = [kappa[x, pl.ds(8 * yb, 8), pl.ds(128 * half, 128)] for half in (0, 1)]
        for c in range(3):
            new = add(centre[c], mul(step, defects[c]))
            for half in (0, 1):
                target[c, x + 1, half, pl.ds(FIRST + 8 * yb, 8), :] = new[half]
                if also_out:
                    moved[c, x, pl.ds(8 * yb, 8), pl.ds(128 * half, 128)] = new[half]
        return centre, defects, shear, mixed

    def first_edge(x, blocks):
        slot = jnp.where(x == 0, 0, jnp.where(x == NX - 1, 1, 2))
        for yb in blocks:
            centre, defects, shear, mixed = sweep_block(v0, v1, x, yb, False)
            step = each(lambda p, q: OMEGA / (SHIFT + ROBIN + 6.0 * p + 2.0 * q), shear, mixed)
            for c in range(3):
                new = add(centre[c], mul(step, defects[c]))
                for half in (0, 1):
                    rimmed[slot, c, half, pl.ds(8 * yb, 8), :] = new[half]
        for side in (0, 1):
            for c in range(3):
                for half in (0, 1):
                    side_send[1, side, c, half, pl.ds(x, 1), :] = rimmed[
                        slot, c, half, pl.ds(0 if side == 0 else NY - 1, 1), :
                    ]

    def first_rest(x, blocks):
        for yb in blocks:
            sweep_block(v0, v1, x, yb, False)

    def second_rest(x, blocks):
        for yb in blocks:
            sweep_block(v1, v2, x, yb, True)

    def second_edge(x, blocks):
        second_rest(x, blocks)
        pack_side(2, v2, x)

    interior(first_rest)
    edges(0, first, v0, first_edge)
    second = messages(1, v1, rimmed.at[0], rimmed.at[1])
    for message in second[:4]:
        message.start()
    pack_corners(
        1,
        lambda dx, dy, c, half: rimmed[
            0 if dx < 0 else 1, c, half, pl.ds(0 if dy < 0 else NY - 1, 1), :
        ],
    )
    for message in second[4:]:
        message.start()

    derive(v1)
    interior(second_rest)
    edges(1, second, v1, second_edge)
    third = messages(2, v2, *faces(v2))
    for message in third[:4]:
        message.start()
    pack_corners(2, field_corner(v2))
    for message in third[4:]:
        message.start()
    derive(v2)

    basis_load.wait()
    total[...] = jnp.zeros_like(total)

    def residual_block(x, yb):
        _, defects, _, _ = block(v2, slope, bend, force, mu, beta, x, yb)
        sums = [None] * 8
        pair = pl.ds(16 * (yb // 2), 16)
        upper = 8 * (yb % 2)
        for c in range(3):
            for half in (0, 1):
                columns = pl.ds(128 * half, 128)
                value = defects[c][half]
                residual[c, x, pl.ds(8 * yb, 8), columns] = value
                value = value.astype(jnp.bfloat16).astype(F32)
                for k in range(8):
                    vector = vectors[k, c, x, pair, columns].astype(F32)[upper : upper + 8]
                    term = vector * value
                    sums[k] = term if sums[k] is None else sums[k] + term
        return sums

    def gather_sums(found):
        for k in range(8):
            part = found[0][k]
            for other in found[1:]:
                part = part + other[k]
            total[k] += part

    def residual_work(x, blocks):
        gather_sums([residual_block(x, yb) for yb in blocks])

    interior(residual_work)
    edges(2, third, v2, residual_work)

    start_lane = 64 * lax.rem(cell, 2) + 8 * place
    spread = jnp.zeros((8, 128), F32)
    for k in range(8):
        spread = jnp.where(lane == start_lane + k, jnp.sum(total[k], axis=1, keepdims=True), spread)
    line[0] = jnp.sum(spread, axis=0, keepdims=True)

    hops = [
        pltpu.make_async_remote_copy(
            src_ref=line.at[0],
            dst_ref=near.at[step],
            send_sem=near_ss.at[step],
            recv_sem=near_rs.at[step],
            device_id=near_peer(step),
            device_id_type=MESH,
        )
        for step in range(7)
    ]
    for hop in hops:
        hop.start()
    joined = line[0]
    rows_load.wait()
    for step, hop in enumerate(hops):
        hop.wait_recv()
        joined = joined + near[step]
    line[1] = joined
    leaps = [
        pltpu.make_async_remote_copy(
            src_ref=line.at[1],
            dst_ref=far.at[step],
            send_sem=far_ss.at[step],
            recv_sem=far_rs.at[step],
            device_id=far_peer(step),
            device_id_type=MESH,
        )
        for step in range(15)
    ]
    for leap in leaps:
        leap.start()

    def product(offset, values):
        dz, dx = offset
        owner = lax.rem(grp + 4 - dz, 4) * 4 + lax.rem(column + 4 - dx, 4)
        columns = pl.ds(pl.multiple_of(lax.div(owner, 2) * 128, 128), 128)
        return rows_r[:, columns] * values

    answer = product((0, 0), joined)
    for message in first + second + third:
        message.wait_send()
    for hop in hops:
        hop.wait_send()
    for step, leap in enumerate(leaps):
        leap.wait_recv()
        answer = answer + product(FAR[step], far[step])
    own_lane = lane == lax.broadcasted_iota(jnp.int32, (8, 128), 0)
    coarse[...] = jnp.sum(
        jnp.where(own_lane, jnp.sum(answer, axis=1, keepdims=True), 0.0), axis=0, keepdims=True
    )
    for leap in leaps:
        leap.wait_send()


def finish(moved, residual, coarse, moved_out, residual_out, coarse_out, store_sem):
    stores = [
        pltpu.make_async_copy(source.at[c], target.at[c], store_sem.at[number, c])
        for number, (source, target) in enumerate(((moved, moved_out), (residual, residual_out)))
        for c in range(3)
    ]
    for store in stores:
        store.start()
    coarse_out[...] = coarse[0, 0:8]
    for store in stores:
        store.wait()


def shards(
    deformation_vector,
    heating_traction,
    heat_level,
    substance_label,
    substance_stiffness_list,
    subregion_spans,
    projection_basis,
    reduced_system_reciprocal,
):
    hbm = pl.BlockSpec(memory_space=pltpu.HBM)
    vmem = pl.BlockSpec(memory_space=pltpu.VMEM)
    smem = pl.BlockSpec(memory_space=pltpu.SMEM)
    field = pltpu.VMEM((3, NX + 2, 2, ROWS, 128), F32)
    scalar = pltpu.VMEM((NX, NY, 256), F32)
    dma = pltpu.SemaphoreType.DMA

    def far(array):
        return pltpu.with_memory_space_constraint(array, pltpu.HBM)

    moved, residual, coarse = pl.pallas_call(
        kernel,
        out_shape=(
            jax.ShapeDtypeStruct((3, NX, NY, 256), F32),
            jax.ShapeDtypeStruct((3, NX, NY, 256), F32),
            jax.ShapeDtypeStruct((1, 128), F32),
        ),
        in_specs=[hbm, hbm, hbm, hbm, hbm, smem, hbm, hbm],
        out_specs=(vmem, vmem, vmem),
        scratch_shapes=[
            field,
            field,
            field,
            field,
            pltpu.VMEM((3, NX, NY, 256), F32),
            pltpu.VMEM((512, 512), jnp.bfloat16),
            pltpu.VMEM((2, 2, 2, NX, 128), F32),
            pltpu.SMEM((2, 4), F32),
            pltpu.VMEM((3, NX, NY, 256), F32),
            scalar,
            pltpu.VMEM((NX, NY, 256), jnp.int32),
            scalar,
            scalar,
            pltpu.VMEM((8, 3, NX, NY, 256), jnp.bfloat16),
            pltpu.VMEM((8, 1024), F32),
            pltpu.VMEM((3, 3, 2, NY, 128), F32),
            pltpu.VMEM((3, 2, 3, 2, NX, 128), F32),
            pltpu.VMEM((3, 2, 3, 2, NX, 128), F32),
            pltpu.VMEM((3, 4, 8, 128), F32),
            pltpu.VMEM((3, 4, 8, 128), F32),
            pltpu.VMEM((8, 8, 128), F32),
            pltpu.VMEM((2, 1, 128), F32),
            pltpu.VMEM((8, 1, 128), F32),
            pltpu.VMEM((16, 1, 128), F32),
            dma((8,)),
            dma((3, 2)),
            dma((3, 2)),
            dma((3, 2)),
            dma((3, 2)),
            dma((3, 4)),
            dma((3, 4)),
            dma((8,)),
            dma((8,)),
            dma((16,)),
            dma((16,)),
        ],
        compiler_params=pltpu.CompilerParams(
            collective_id=0, has_side_effects=True, vmem_limit_bytes=46 * 1024 * 1024
        ),
    )(
        far(deformation_vector),
        far(heating_traction),
        far(heat_level),
        far(substance_label),
        far(substance_stiffness_list.T),
        subregion_spans,
        far(projection_basis),
        far(reduced_system_reciprocal),
    )
    return pl.pallas_call(
        finish,
        out_shape=(
            jax.ShapeDtypeStruct((3, NX, NY, 256), F32),
            jax.ShapeDtypeStruct((3, NX, NY, 256), F32),
            jax.ShapeDtypeStruct((8,), F32),
        ),
        in_specs=[vmem, vmem, vmem],
        out_specs=(hbm, hbm, vmem),
        scratch_shapes=[dma((2, 3))],
        compiler_params=pltpu.CompilerParams(vmem_limit_bytes=1024 * 1024),
    )(moved, residual, coarse)


def solution(mesh):
    placed = (
        P(None, "grp", "sub", None),
        P(None, "grp", "sub", None),
        P("grp", "sub", None),
        P("grp", "sub", None),
        P(),
        P("grp", "sub"),
        P(None, None, "grp", "sub", None),
        P(("grp", "sub"), None),
    )
    return jax.shard_map(
        shards,
        mesh=mesh,
        in_specs=placed,
        out_specs=(P(None, "grp", "sub", None), P(None, "grp", "sub", None), P(("grp", "sub"))),
        check_vma=False,
    )
```
